256 devices in a mesh: blk: 32 (over z, x_lo, core), narrow: 8 (over x_hi, y).
Axes of the slice: x: 4 (x_hi: 2, x_lo: 2; x = x_hi * 2 + x_lo), y: 4, z: 8, core: 2. Of those that a mesh axis runs over, the one named last changes fastest.
Arguments:
- tensor: float32 [448, 128, 4224], P('blk', 'narrow'), may hold values from -25 to 25
- factor_two: float32 [128, 64], replicated, may hold values from -0.5 to 0.5
- factor_three: float32 [16, 16], replicated, may hold values from -1.5 to 1.5
- factor_four: float32 [33, 16], replicated, may hold values from -1 to 1
- factor_five: float32 [8, 8], replicated, may hold values from -2 to 2
Outputs:
- gram_matrix: float32 [448, 448], P('blk', 'narrow')
The draws below stay inside these ranges and needn't reach their ends.
All inputs are finite; a program needn't handle non-finite values.
Results may differ from the reference program's by a relative error of at most 0.0003.
Values may be sent and summed in bfloat16 or wider, within the bound.
No kernel may reach another device: no remote copies, remote signals or barrier semaphores. Data moves between devices by JAX's collectives and lax.ppermute only.
A program may use at most 128 MiB of HBM per device.

```python
import math
import jax
import jax.numpy as jnp
from jax import lax

ROWS_DEV = 14
I3 = 16
I4 = 33
I5 = 8
R2 = 64
R3 = 16
R4 = 16
R5 = 8
I1 = 448
I2 = 128
CELLS = 4224


def draw_tensor(key, part):
    key = jax.random.fold_in(key, 7)
    key_noise, key_row, key_cell = jax.random.split(key, 3)
    row_scale = jnp.exp(jax.random.uniform(key_row, (I1, 1, 1), jnp.float32, -1.15, 1.15))
    cell_scale = jnp.exp(jax.random.uniform(key_cell, (1, 1, CELLS), jnp.float32, -0.35, 0.35))
    noise = jnp.clip(jax.random.normal(key_noise, (I1, I2, CELLS), jnp.float32), -5.0, 5.0)
    return (noise * row_scale * cell_scale).astype(jnp.float32)


def gaussian(stream_key, extent, deviation, limit, kind=jnp.bfloat16):
    entries = deviation * jax.random.normal(stream_key, extent, jnp.float32)
    return jnp.clip(entries, min=-limit, max=limit).astype(kind)


def setup_inputs(seed: int = 0) -> dict:
    keys = jax.random.split(jax.random.key(seed), 6)
    return {
        "tensor": draw_tensor(jax.random.fold_in(keys[5], 71), 0),
        "factor_two": gaussian(keys[1], (I2, R2), I2 ** -0.5, 0.5, jnp.float32),
        "factor_three": gaussian(keys[2], (I3, R3), I3 ** -0.5, 1.5, jnp.float32),
        "factor_four": gaussian(keys[3], (I4, R4), I4 ** -0.5, 1.0, jnp.float32),
        "factor_five": gaussian(keys[4], (I5, R5), I5 ** -0.5, 2.0, jnp.float32),
    }


def squeeze_cells(slab_rows, factor_three, factor_four, factor_five):
    row_count, depth_rows, cell_count = slab_rows.shape
    third_size = factor_three.shape[0]
    third_rank = factor_three.shape[1]
    pair_factor = (factor_four[:, None, :, None] * factor_five[None, :, None, :]).reshape(factor_four.shape[0] * factor_five.shape[0], factor_four.shape[1] * factor_five.shape[1])
    flat_cells = slab_rows.reshape(row_count * depth_rows * third_size, cell_count // third_size)
    inner_cells = jnp.dot(flat_cells, pair_factor, precision=lax.Precision.HIGHEST, preferred_element_type=jnp.float32)
    inner_cells = inner_cells.reshape(row_count * depth_rows, third_size, pair_factor.shape[1])
    outer_cells = jnp.einsum('mac,ar->mrc', inner_cells, factor_three, precision=lax.Precision.HIGHEST)
    return outer_cells.reshape(row_count, depth_rows, third_rank * pair_factor.shape[1])

def reference(tensor, factor_two, factor_three, factor_four, factor_five):
    slabs = tensor.reshape(I1 // ROWS_DEV, ROWS_DEV, I2, CELLS)

    def project_block(slab_rows):
        reduced = squeeze_cells(slab_rows, factor_three, factor_four, factor_five)
        core_rows = jnp.einsum('mjk,jr->mrk', reduced, factor_two, precision=lax.Precision.HIGHEST)
        return core_rows.astype(jnp.bfloat16).reshape(ROWS_DEV, -1)
    rounded = lax.map(project_block, slabs).reshape(I1, -1)
    gram_block = jnp.dot(rounded, rounded.T, preferred_element_type=jnp.float32)
    return gram_block * (1.0 / math.sqrt(rounded.shape[1]))
```

```python
import math

import jax
import jax.numpy as jnp
from jax import lax
from jax.experimental import pallas as pl
from jax.experimental.pallas import tpu as pltpu
from jax.sharding import Mesh, PartitionSpec as P

F32 = jnp.float32
BF16 = jnp.bfloat16
ROWS, DEPTH, I3, I4, I5 = 14, 16, 16, 33, 8
R2, R3, R4, R5 = 64, 16, 16, 8
CELLS = I3 * I4 * I5
INNER = I4 * I5
PAIR = R4 * R5
PAD = 16
ROWS_STEP = 2
Z, XL, CORE, XH, Y = 8, 2, 2, 2, 4
NARROW = XH * Y
GROUPS = Z * XL
VMEM_LIMIT = 32 * 1024 * 1024


def split(value):
    high = value.astype(BF16)
    return high, (value - high.astype(F32)).astype(BF16)


def dot(left, right):
    return lax.dot_general(left, right, (((1,), (0,)), ((), ())), preferred_element_type=F32)


def exact_dot(left, right, dims):
    return lax.dot_general(
        left, right, (dims, ((), ())), precision=lax.Precision.HIGHEST, preferred_element_type=F32
    )


def squeeze_kernel(t_ref, f3_ref, f4t_ref, f5_ref, out_ref, pair_hl, mix_h, mix_l):
    step = pl.program_id(0)

    @pl.when(step == 0)
    def _():
        lane = lax.broadcasted_iota(jnp.int32, (R4, PAIR), 1)
        row = lax.broadcasted_iota(jnp.int32, (R4, PAIR), 0)
        spread_four = (lane // R5 == row).astype(F32)
        lane = lax.broadcasted_iota(jnp.int32, (R5, PAIR), 1)
        row = lax.broadcasted_iota(jnp.int32, (R5, PAIR), 0)
        spread_five = (lane % R5 == row).astype(F32)
        four = exact_dot(f4t_ref[...], spread_four, ((0,), (0,)))
        five = exact_dot(f5_ref[...], spread_five, ((1,), (0,)))
        pair = (four[:, None, :] * five[None, :, :]).reshape(INNER, PAIR)
        high, low = split(pair)
        pair_hl[:, :PAIR] = high
        pair_hl[:, PAIR:] = low
        size = R3 * DEPTH
        a_row = lax.broadcasted_iota(jnp.int32, (size, I3), 0) // DEPTH
        a_col = lax.broadcasted_iota(jnp.int32, (size, I3), 1)
        pick = (a_row == a_col).astype(F32)
        rows = exact_dot(pick, f3_ref[...], ((1,), (1,)))
        full = exact_dot(rows, pick, ((1,), (1,)))
        same = (
            lax.broadcasted_iota(jnp.int32, (size, size), 0) % DEPTH
            == lax.broadcasted_iota(jnp.int32, (size, size), 1) % DEPTH
        )
        high, low = split(jnp.where(same, full, 0.0))
        mix_h[...] = high
        mix_l[...] = low

    for local in range(ROWS_STEP):
        high, low = split(t_ref[local])
        left_h = jnp.concatenate([high[:, a * INNER:(a + 1) * INNER] for a in range(I3)], axis=0)
        left_l = jnp.concatenate([low[:, a * INNER:(a + 1) * INNER] for a in range(I3)], axis=0)
        both = dot(left_h, pair_hl[...])
        inner = both[:, :PAIR] + (both[:, PAIR:] + dot(left_l, pair_hl[:, :PAIR]))
        inner_h, inner_l = split(inner)
        both = dot(mix_h[...], jnp.concatenate([inner_h, inner_l], axis=1))
        outer = both[:, :PAIR] + (both[:, PAIR:] + dot(mix_l[...], inner_h))
        out_ref[:, step * ROWS_STEP + local] = outer.reshape(NARROW, -1, PAIR).astype(out_ref.dtype)


def squeeze(tensor, f3, f4t, f5):
    size = R3 * DEPTH
    return pl.pallas_call(
        squeeze_kernel,
        grid=(ROWS // ROWS_STEP,),
        in_specs=[
            pl.BlockSpec((ROWS_STEP, DEPTH, CELLS), lambda s: (s, 0, 0)),
            pl.BlockSpec((I3, R3), lambda s: (0, 0)),
            pl.BlockSpec((R4, I4), lambda s: (0, 0)),
            pl.BlockSpec((I5, R5), lambda s: (0, 0)),
        ],
        out_specs=pl.BlockSpec((NARROW, ROWS, size // NARROW, PAIR), lambda s: (0, 0, 0, 0)),
        out_shape=jax.ShapeDtypeStruct((NARROW, ROWS, size // NARROW, PAIR), BF16),
        scratch_shapes=[
            pltpu.VMEM((INNER, 2 * PAIR), BF16),
            pltpu.VMEM((size, size), BF16),
            pltpu.VMEM((size, size), BF16),
        ],
        compiler_params=pltpu.CompilerParams(vmem_limit_bytes=VMEM_LIMIT),
    )(tensor, f3, f4t, f5)


def expand_kernel(x_ref, f2t_ref, out_ref, rows_ref):
    high, low = split(f2t_ref[...])
    left = jnp.concatenate([high, low], axis=0)
    width = 2 * PAIR
    for i in range(ROWS):
        piece = x_ref[:, i]
        right = jnp.concatenate(
            [piece[:, h * DEPTH:(h + 1) * DEPTH].reshape(NARROW * DEPTH, PAIR) for h in range(2)], axis=1
        )
        both = dot(left, right)
        core = both[:R2] + both[R2:]
        for h in range(2):
            rows_ref[h, pl.ds(i, R2, stride=PAD), :] = core[:, h * PAIR:(h + 1) * PAIR]
    keep = lax.broadcasted_iota(jnp.int32, (R2, PAD, PAIR), 1) < ROWS
    for h in range(2):
        block = jnp.where(keep, rows_ref[h].reshape(R2, PAD, PAIR), 0.0)
        out_ref[:, :, :, h * PAIR:(h + 1) * PAIR] = block.astype(BF16).reshape(GROUPS, -1, PAD, PAIR)


def expand(gathered, f2t):
    return pl.pallas_call(
        expand_kernel,
        out_shape=jax.ShapeDtypeStruct((GROUPS, R2 // GROUPS, PAD, 2 * PAIR), BF16),
        scratch_shapes=[pltpu.VMEM((2, R2 * PAD, PAIR), F32)],
        compiler_params=pltpu.CompilerParams(vmem_limit_bytes=VMEM_LIMIT),
    )(gathered, f2t)


def gram_kernel(x_ref, out_ref):
    own = lax.axis_index("core")
    total = None
    for q in range(R2 // GROUPS):
        left = x_ref[own, :, q].reshape(GROUPS * PAD, 2 * PAIR)
        right = jnp.concatenate(
            [x_ref[c, g, q] for g in range(GROUPS) for c in range(CORE)], axis=0
        )
        part = lax.dot_general(left, right, (((1,), (1,)), ((), ())), preferred_element_type=F32)
        total = part if total is None else total + part
    first = lax.broadcasted_iota(jnp.int32, (8, 128), 1) < 64
    for g in range(GROUPS):
        for n in range(0, NARROW, 2):
            top = total[g * PAD:g * PAD + 8, n * 64:n * 64 + 128]
            bottom = total[g * PAD + 8:(g + 1) * PAD, n * 64:n * 64 + 128]
            out_ref[g * NARROW + n] = jnp.where(first, top, pltpu.roll(bottom, 64, 1))
            out_ref[g * NARROW + n + 1] = jnp.where(first, pltpu.roll(top, 64, 1), bottom)


def gram(blocks):
    return pl.pallas_call(
        gram_kernel,
        out_shape=jax.ShapeDtypeStruct((GROUPS * NARROW, 8, 128), F32),
        compiler_params=pltpu.CompilerParams(vmem_limit_bytes=VMEM_LIMIT),
    )(blocks)


def finish_kernel(x_ref, out_ref):
    scale = 1.0 / math.sqrt(R2 * R3 * R4 * R5)
    total = jnp.sum(x_ref[...], axis=0) * scale
    rows = jnp.concatenate([total[:, :64], total[:, 64:]], axis=0)[:ROWS]
    out_ref[...] = jnp.concatenate([rows[:, g * PAD:g * PAD + ROWS] for g in range(4)], axis=1)


def finish(parts):
    return pl.pallas_call(
        finish_kernel,
        out_shape=jax.ShapeDtypeStruct((ROWS, 4 * ROWS), F32),
        compiler_params=pltpu.CompilerParams(vmem_limit_bytes=VMEM_LIMIT),
    )(parts)


def per_device(tensor, f2, f3, f4, f5):
    with jax.named_scope("squeeze"):
        reduced = squeeze(tensor, f3, f4.T, f5)
    with jax.named_scope("depth_exchange"):
        gathered = lax.all_to_all(reduced, ("x_hi", "y"), 0, 0, tiled=True)
    with jax.named_scope("expand"):
        core = expand(gathered, f2.T)
    with jax.named_scope("row_exchange"):
        rows = lax.all_to_all(core, ("z", "x_lo"), 0, 0, tiled=True)
    with jax.named_scope("core_gather"):
        both = lax.all_gather(rows, "core")
    with jax.named_scope("gram"):
        parts = gram(both)
    with jax.named_scope("gram_exchange"):
        parts = lax.all_to_all(parts, ("z", "x_lo", "x_hi", "y"), 0, 0, tiled=True)
    with jax.named_scope("finish"):
        return finish(parts)


def solution(mesh):
    fine = Mesh(
        mesh.devices.reshape(Z, XL, CORE, XH, Y), ("z", "x_lo", "core", "x_hi", "y")
    )
    blk, narrow = ("z", "x_lo", "core"), ("x_hi", "y")
    return jax.shard_map(
        per_device,
        mesh=fine,
        in_specs=(P(blk, narrow, None), P(), P(), P(), P()),
        out_specs=P(blk, narrow),
        check_vma=False,
    )
```

```python
import math

import jax
import jax.numpy as jnp
from jax import lax
from jax.experimental import pallas as pl
from jax.experimental.pallas import tpu as pltpu
from jax.sharding import Mesh, PartitionSpec as P

F32 = jnp.float32
BF16 = jnp.bfloat16
ROWS, DEPTH, I3, I4, I5 = 14, 16, 16, 33, 8
R2, R3, R4, R5 = 64, 16, 16, 8
CELLS = I3 * I4 * I5
INNER = I4 * I5
PAIR = R4 * R5
PAD = 16
ROWS_STEP = 2
Z, XL, CORE, XH, Y = 8, 2, 2, 2, 4
NARROW = XH * Y
GROUPS = Z * XL
VMEM_LIMIT = 32 * 1024 * 1024


def split(value):
    high = value.astype(BF16)
    return high, (value - high.astype(F32)).astype(BF16)


def dot(left, right):
    return lax.dot_general(left, right, (((1,), (0,)), ((), ())), preferred_element_type=F32)


def exact_dot(left, right, dims):
    return lax.dot_general(
        left, right, (dims, ((), ())), precision=lax.Precision.HIGHEST, preferred_element_type=F32
    )


def squeeze_kernel(t_ref, f3_ref, f4t_ref, f5_ref, out_ref, pair_hl, mix_h, mix_l):
    step = pl.program_id(0)

    @pl.when(step == 0)
    def _():
        lane = lax.broadcasted_iota(jnp.int32, (R4, PAIR), 1)
        row = lax.broadcasted_iota(jnp.int32, (R4, PAIR), 0)
        spread_four = (lane // R5 == row).astype(F32)
        lane = lax.broadcasted_iota(jnp.int32, (R5, PAIR), 1)
        row = lax.broadcasted_iota(jnp.int32, (R5, PAIR), 0)
        spread_five = (lane % R5 == row).astype(F32)
        four = exact_dot(f4t_ref[...], spread_four, ((0,), (0,)))
        five = exact_dot(f5_ref[...], spread_five, ((1,), (0,)))
        pair = (four[:, None, :] * five[None, :, :]).reshape(INNER, PAIR)
        high, low = split(pair)
        pair_hl[:, :PAIR] = high
        pair_hl[:, PAIR:] = low
        size = R3 * DEPTH
        a_row = lax.broadcasted_iota(jnp.int32, (size, I3), 0) // DEPTH
        a_col = lax.broadcasted_iota(jnp.int32, (size, I3), 1)
        pick = (a_row == a_col).astype(F32)
        rows = exact_dot(pick, f3_ref[...], ((1,), (1,)))
        full = exact_dot(rows, pick, ((1,), (1,)))
        same = (
            lax.broadcasted_iota(jnp.int32, (size, size), 0) % DEPTH
            == lax.broadcasted_iota(jnp.int32, (size, size), 1) % DEPTH
        )
        high, low = split(jnp.where(same, full, 0.0))
        mix_h[...] = high
        mix_l[...] = low

    for local in range(ROWS_STEP):
        high, low = split(t_ref[local])
        left_h = jnp.concatenate([high[:, a * INNER:(a + 1) * INNER] for a in range(I3)], axis=0)
        left_l = jnp.concatenate([low[:, a * INNER:(a + 1) * INNER] for a in range(I3)], axis=0)
        both = dot(left_h, pair_hl[...])
        inner = both[:, :PAIR] + (both[:, PAIR:] + dot(left_l, pair_hl[:, :PAIR]))
        inner_h, inner_l = split(inner)
        both = dot(mix_h[...], jnp.concatenate([inner_h, inner_l], axis=1))
        outer = both[:, :PAIR] + (both[:, PAIR:] + dot(mix_l[...], inner_h))
        out_ref[:, step * ROWS_STEP + local] = outer.reshape(NARROW, -1, PAIR).astype(out_ref.dtype)


def squeeze(tensor, f3, f4t, f5):
    size = R3 * DEPTH
    return pl.pallas_call(
        squeeze_kernel,
        grid=(ROWS // ROWS_STEP,),
        in_specs=[
            pl.BlockSpec((ROWS_STEP, DEPTH, CELLS), lambda s: (s, 0, 0)),
            pl.BlockSpec((I3, R3), lambda s: (0, 0)),
            pl.BlockSpec((R4, I4), lambda s: (0, 0)),
            pl.BlockSpec((I5, R5), lambda s: (0, 0)),
        ],
        out_specs=pl.BlockSpec((NARROW, ROWS, size // NARROW, PAIR), lambda s: (0, 0, 0, 0)),
        out_shape=jax.ShapeDtypeStruct((NARROW, ROWS, size // NARROW, PAIR), BF16),
        scratch_shapes=[
            pltpu.VMEM((INNER, 2 * PAIR), BF16),
            pltpu.VMEM((size, size), BF16),
            pltpu.VMEM((size, size), BF16),
        ],
        compiler_params=pltpu.CompilerParams(vmem_limit_bytes=VMEM_LIMIT),
    )(tensor, f3, f4t, f5)


def expand_kernel(x_ref, f2t_ref, out_ref, rows_ref):
    high, low = split(f2t_ref[...])
    left = jnp.concatenate([high, low], axis=0)
    width = 2 * PAIR
    for i in range(ROWS):
        piece = x_ref[:, i]
        right = jnp.concatenate(
            [piece[:, h * DEPTH:(h + 1) * DEPTH].reshape(NARROW * DEPTH, PAIR) for h in range(2)], axis=1
        )
        both = dot(left, right)
        core = both[:R2] + both[R2:]
        for h in range(2):
            rows_ref[h, pl.ds(i, R2, stride=PAD), :] = core[:, h * PAIR:(h + 1) * PAIR]
    keep = lax.broadcasted_iota(jnp.int32, (R2, PAD, PAIR), 1) < ROWS
    for h in range(2):
        block = jnp.where(keep, rows_ref[h].reshape(R2, PAD, PAIR), 0.0)
        out_ref[:, :, :, h * PAIR:(h + 1) * PAIR] = block.astype(BF16).reshape(GROUPS, -1, PAD, PAIR)


def expand(gathered, f2t):
    return pl.pallas_call(
        expand_kernel,
        out_shape=jax.ShapeDtypeStruct((GROUPS, R2 // GROUPS, PAD, 2 * PAIR), BF16),
        scratch_shapes=[pltpu.VMEM((2, R2 * PAD, PAIR), F32)],
        compiler_params=pltpu.CompilerParams(vmem_limit_bytes=VMEM_LIMIT),
    )(gathered, f2t)


def gram_kernel(own_ref, other_ref, out_ref):
    total = None
    for q in range(R2 // GROUPS):
        left = own_ref[:, q].reshape(GROUPS * PAD, 2 * PAIR)
        right = jnp.concatenate(
            [ref[g, q] for g in range(GROUPS) for ref in (own_ref, other_ref)], axis=0
        )
        part = lax.dot_general(left, right, (((1,), (1,)), ((), ())), preferred_element_type=F32)
        total = part if total is None else total + part
    first = lax.broadcasted_iota(jnp.int32, (8, 128), 1) < 64
    for g in range(GROUPS):
        for n in range(0, NARROW, 2):
            top = total[g * PAD:g * PAD + 8, n * 64:n * 64 + 128]
            bottom = total[g * PAD + 8:(g + 1) * PAD, n * 64:n * 64 + 128]
            out_ref[g * NARROW + n] = jnp.where(first, top, pltpu.roll(bottom, 64, 1))
            out_ref[g * NARROW + n + 1] = jnp.where(first, pltpu.roll(top, 64, 1), bottom)


def gram(own, other):
    return pl.pallas_call(
        gram_kernel,
        out_shape=jax.ShapeDtypeStruct((GROUPS * NARROW, 8, 128), F32),
        compiler_params=pltpu.CompilerParams(vmem_limit_bytes=VMEM_LIMIT),
    )(own, other)


def finish_kernel(x_ref, out_ref):
    scale = 1.0 / math.sqrt(R2 * R3 * R4 * R5)
    total = jnp.sum(x_ref[...], axis=0) * scale
    rows = jnp.concatenate([total[:, :64], total[:, 64:]], axis=0)[:ROWS]
    group = [rows[:, g * PAD:g * PAD + ROWS] for g in range(4)]
    first = lax.axis_index("core") == 0
    out_ref[...] = jnp.where(
        first, jnp.concatenate(group, axis=1), jnp.concatenate([group[g ^ 1] for g in range(4)], axis=1)
    )


def finish(parts):
    return pl.pallas_call(
        finish_kernel,
        out_shape=jax.ShapeDtypeStruct((ROWS, 4 * ROWS), F32),
        compiler_params=pltpu.CompilerParams(vmem_limit_bytes=VMEM_LIMIT),
    )(parts)


def per_device(tensor, f2, f3, f4, f5):
    with jax.named_scope("squeeze"):
        reduced = squeeze(tensor, f3, f4.T, f5)
    with jax.named_scope("depth_exchange"):
        gathered = lax.all_to_all(reduced, ("x_hi", "y"), 0, 0, tiled=True)
    with jax.named_scope("expand"):
        core = expand(gathered, f2.T)
    with jax.named_scope("row_exchange"):
        rows = lax.all_to_all(core, ("z", "x_lo"), 0, 0, tiled=True)
    with jax.named_scope("core_swap"):
        other = lax.ppermute(rows, "core", [(0, 1), (1, 0)])
    with jax.named_scope("gram"):
        parts = gram(rows, other)
    with jax.named_scope("gram_exchange"):
        parts = lax.all_to_all(parts, ("z", "x_lo", "x_hi", "y"), 0, 0, tiled=True)
    with jax.named_scope("finish"):
        return finish(parts)


def solution(mesh):
    fine = Mesh(
        mesh.devices.reshape(Z, XL, CORE, XH, Y), ("z", "x_lo", "core", "x_hi", "y")
    )
    blk, narrow = ("z", "x_lo", "core"), ("x_hi", "y")
    return jax.shard_map(
        per_device,
        mesh=fine,
        in_specs=(P(blk, narrow, None), P(), P(), P(), P()),
        out_specs=P(blk, narrow),
        check_vma=False,
    )
```

```python
import math

import jax
import jax.numpy as jnp
from jax import lax
from jax.experimental import pallas as pl
from jax.experimental.pallas import tpu as pltpu
from jax.sharding import Mesh, PartitionSpec as P

F32 = jnp.float32
BF16 = jnp.bfloat16
ROWS, DEPTH, I3, I4, I5 = 14, 16, 16, 33, 8
R2, R3, R4, R5 = 64, 16, 16, 8
CELLS = I3 * I4 * I5
INNER = I4 * I5
PAIR = R4 * R5
MAIN = 256
PAD = 16
ROWS_STEP = 2
Z, XL, CORE, XH, Y = 8, 2, 2, 2, 4
NARROW = XH * Y
GROUPS = Z * XL
VMEM_LIMIT = 32 * 1024 * 1024


def split(value):
    high = value.astype(BF16)
    return high, (value - high.astype(F32)).astype(BF16)


def dot(left, right):
    return lax.dot_general(left, right, (((1,), (0,)), ((), ())), preferred_element_type=F32)


def exact_dot(left, right, dims):
    return lax.dot_general(
        left, right, (dims, ((), ())), precision=lax.Precision.HIGHEST, preferred_element_type=F32
    )


def squeeze_kernel(t_hbm, f3_hbm, f4t_hbm, f5_hbm, out_ref, t_ref, f3_ref, f4t_ref, f5_ref, main_h, main_l, rest, mix_h, mix_l, sems):
    small = [
        pltpu.make_async_copy(src, dst, sems.at[ROWS + n])
        for n, (src, dst) in enumerate(((f3_hbm, f3_ref), (f4t_hbm, f4t_ref), (f5_hbm, f5_ref)))
    ]
    loads = [pltpu.make_async_copy(t_hbm.at[i], t_ref.at[i], sems.at[i]) for i in range(ROWS)]
    for copy in small + loads:
        copy.start()
    for copy in small:
        copy.wait()

    lane = lax.broadcasted_iota(jnp.int32, (R4, PAIR), 1)
    row = lax.broadcasted_iota(jnp.int32, (R4, PAIR), 0)
    spread_four = (lane // R5 == row).astype(F32)
    lane = lax.broadcasted_iota(jnp.int32, (R5, PAIR), 1)
    row = lax.broadcasted_iota(jnp.int32, (R5, PAIR), 0)
    spread_five = (lane % R5 == row).astype(F32)
    four = exact_dot(f4t_ref[...], spread_four, ((0,), (0,)))
    five = exact_dot(f5_ref[...], spread_five, ((1,), (0,)))
    pair = (four[:, None, :] * five[None, :, :]).reshape(INNER, PAIR)
    high, low = split(pair)
    main_h[:, :PAIR] = high
    main_h[:, PAIR:] = low
    tail_h, tail_l = high[MAIN:], low[MAIN:]
    rest[...] = jnp.concatenate(
        [
            jnp.concatenate([tail_h, tail_l], axis=1),
            jnp.concatenate([tail_h, jnp.zeros_like(tail_l)], axis=1),
        ],
        axis=0,
    )
    size = R3 * DEPTH
    a_row = lax.broadcasted_iota(jnp.int32, (size, I3), 0) // DEPTH
    a_col = lax.broadcasted_iota(jnp.int32, (size, I3), 1)
    pick = (a_row == a_col).astype(F32)
    rows = exact_dot(pick, f3_ref[...], ((1,), (1,)))
    full = exact_dot(rows, pick, ((1,), (1,)))
    same = (
        lax.broadcasted_iota(jnp.int32, (size, size), 0) % DEPTH
        == lax.broadcasted_iota(jnp.int32, (size, size), 1) % DEPTH
    )
    high, low = split(jnp.where(same, full, 0.0))
    mix_h[...] = high
    mix_l[...] = low

    size_in = R3 * DEPTH
    for base in range(0, ROWS, 7):
        group = range(base, base + 7)
        for i in group:
            loads[i].wait()
        halves = [split(t_ref[i]) for i in group]
        starts = [a * INNER for a in range(I3)]
        left_h = jnp.concatenate([h[:, s:s + INNER] for h, _ in halves for s in starts], axis=0)
        left_l = jnp.concatenate([l[:, s:s + INNER] for _, l in halves for s in starts], axis=0)
        both = dot(left_h, main_h[...])
        stack = both[:, :PAIR] + (both[:, PAIR:] + dot(left_l, main_h[:, :PAIR]))
        for n, i in enumerate(group):
            inner_h, inner_l = split(stack[n * size_in:(n + 1) * size_in])
            both = dot(mix_h[...], jnp.concatenate([inner_h, inner_l], axis=1))
            outer = both[:, :PAIR] + (both[:, PAIR:] + dot(mix_l[...], inner_h))
            out_ref[:, i] = outer.reshape(NARROW, -1, PAIR).astype(out_ref.dtype)


def squeeze(tensor, f3, f4t, f5):
    size = R3 * DEPTH
    hbm = pl.BlockSpec(memory_space=pltpu.MemorySpace.HBM)
    return pl.pallas_call(
        squeeze_kernel,
        in_specs=[hbm] * 4,
        out_shape=jax.ShapeDtypeStruct((NARROW, ROWS, size // NARROW, PAIR), BF16),
        scratch_shapes=[
            pltpu.VMEM((ROWS, DEPTH, CELLS), F32),
            pltpu.VMEM((I3, R3), F32),
            pltpu.VMEM((R4, I4), F32),
            pltpu.VMEM((I5, R5), F32),
            pltpu.VMEM((INNER, 2 * PAIR), BF16),
            pltpu.VMEM((MAIN, PAIR), BF16),
            pltpu.VMEM((2 * (INNER - MAIN), 2 * PAIR), BF16),
            pltpu.VMEM((size, size), BF16),
            pltpu.VMEM((size, size), BF16),
            pltpu.SemaphoreType.DMA((ROWS + 3,)),
        ],
        compiler_params=pltpu.CompilerParams(vmem_limit_bytes=61 * 1024 * 1024),
    )(tensor, f3, f4t, f5)


def expand_kernel(x_ref, f2t_ref, out_ref, rows_ref):
    high, low = split(f2t_ref[...])
    left = jnp.concatenate([high, low], axis=0)
    width = 2 * PAIR
    for i in range(ROWS):
        piece = x_ref[:, i]
        right = jnp.concatenate(
            [piece[:, h * DEPTH:(h + 1) * DEPTH].reshape(NARROW * DEPTH, PAIR) for h in range(2)], axis=1
        )
        both = dot(left, right)
        core = both[:R2] + both[R2:]
        for h in range(2):
            rows_ref[h, pl.ds(i, R2, stride=PAD), :] = core[:, h * PAIR:(h + 1) * PAIR]
    keep = lax.broadcasted_iota(jnp.int32, (R2, PAD, PAIR), 1) < ROWS
    for h in range(2):
        block = jnp.where(keep, rows_ref[h].reshape(R2, PAD, PAIR), 0.0)
        out_ref[:, :, :, h * PAIR:(h + 1) * PAIR] = block.astype(BF16).reshape(GROUPS, -1, PAD, PAIR)


def expand(gathered, f2t):
    return pl.pallas_call(
        expand_kernel,
        out_shape=jax.ShapeDtypeStruct((GROUPS, R2 // GROUPS, PAD, 2 * PAIR), BF16),
        scratch_shapes=[pltpu.VMEM((2, R2 * PAD, PAIR), F32)],
        compiler_params=pltpu.CompilerParams(vmem_limit_bytes=VMEM_LIMIT),
    )(gathered, f2t)


def gram_kernel(own_ref, other_ref, out_ref):
    total = None
    for q in range(R2 // GROUPS):
        left = own_ref[:, q].reshape(GROUPS * PAD, 2 * PAIR)
        right = jnp.concatenate(
            [ref[g, q] for g in range(GROUPS) for ref in (own_ref, other_ref)], axis=0
        )
        part = lax.dot_general(left, right, (((1,), (1,)), ((), ())), preferred_element_type=F32)
        total = part if total is None else total + part
    first = lax.broadcasted_iota(jnp.int32, (8, 128), 1) < 64
    for g in range(GROUPS):
        for n in range(0, NARROW, 2):
            top = total[g * PAD:g * PAD + 8, n * 64:n * 64 + 128]
            bottom = total[g * PAD + 8:(g + 1) * PAD, n * 64:n * 64 + 128]
            out_ref[g * NARROW + n] = jnp.where(first, top, pltpu.roll(bottom, 64, 1))
            out_ref[g * NARROW + n + 1] = jnp.where(first, pltpu.roll(top, 64, 1), bottom)


def gram(own, other):
    return pl.pallas_call(
        gram_kernel,
        out_shape=jax.ShapeDtypeStruct((GROUPS * NARROW, 8, 128), F32),
        compiler_params=pltpu.CompilerParams(vmem_limit_bytes=VMEM_LIMIT),
    )(own, other)


def finish_kernel(x_ref, out_ref):
    scale = 1.0 / math.sqrt(R2 * R3 * R4 * R5)
    total = jnp.sum(x_ref[...], axis=0) * scale
    rows = jnp.concatenate([total[:, :64], total[:, 64:]], axis=0)[:ROWS]
    group = [rows[:, g * PAD:g * PAD + ROWS] for g in range(4)]
    first = lax.axis_index("core") == 0
    out_ref[...] = jnp.where(
        first, jnp.concatenate(group, axis=1), jnp.concatenate([group[g ^ 1] for g in range(4)], axis=1)
    )


def finish(parts):
    return pl.pallas_call(
        finish_kernel,
        out_shape=jax.ShapeDtypeStruct((ROWS, 4 * ROWS), F32),
        compiler_params=pltpu.CompilerParams(vmem_limit_bytes=VMEM_LIMIT),
    )(parts)


def per_device(tensor, f2, f3, f4, f5):
    with jax.named_scope("squeeze"):
        reduced = squeeze(tensor, f3, f4.T, f5)
    with jax.named_scope("depth_exchange"):
        gathered = lax.all_to_all(reduced, ("x_hi", "y"), 0, 0, tiled=True)
    with jax.named_scope("expand"):
        core = expand(gathered, f2.T)
    with jax.named_scope("row_exchange"):
        rows = lax.all_to_all(core, ("z", "x_lo"), 0, 0, tiled=True)
    with jax.named_scope("core_swap"):
        other = lax.ppermute(rows, "core", [(0, 1), (1, 0)])
    with jax.named_scope("gram"):
        parts = gram(rows, other)
    with jax.named_scope("gram_exchange"):
        parts = lax.all_to_all(parts, ("z", "x_lo", "x_hi", "y"), 0, 0, tiled=True)
    with jax.named_scope("finish"):
        return finish(parts)


def solution(mesh):
    fine = Mesh(
        mesh.devices.reshape(Z, XL, CORE, XH, Y), ("z", "x_lo", "core", "x_hi", "y")
    )
    blk, narrow = ("z", "x_lo", "core"), ("x_hi", "y")
    return jax.shard_map(
        per_device,
        mesh=fine,
        in_specs=(P(blk, narrow, None), P(), P(), P(), P()),
        out_specs=P(blk, narrow),
        check_vma=False,
    )
```

```python
import math

import jax
import jax.numpy as jnp
from jax import lax
from jax.experimental import pallas as pl
from jax.experimental.pallas import tpu as pltpu
from jax.sharding import Mesh, PartitionSpec as P

F32 = jnp.float32
BF16 = jnp.bfloat16
F16 = jnp.float16
ROWS, DEPTH, I3, I4, I5 = 14, 16, 16, 33, 8
R2, R3, R4, R5 = 64, 16, 16, 8
CELLS = I3 * I4 * I5
INNER = I4 * I5
PAIR = R4 * R5
MAIN = 256
WIDE = R3 * DEPTH // 8
PAD = 16
ROWS_STEP = 2
Z, XL, CORE, XH, Y = 8, 2, 2, 2, 4
NARROW = XH * Y
GROUPS = Z * XL
VMEM_LIMIT = 32 * 1024 * 1024


def split(value):
    high = value.astype(BF16)
    return high, (value - high.astype(F32)).astype(BF16)


def dot(left, right):
    return lax.dot_general(left, right, (((1,), (0,)), ((), ())), preferred_element_type=F32)


def exponent(peak):
    return jnp.floor(jnp.log2(jnp.maximum(peak, 1e-30))) - 14.0


def exact_dot(left, right, dims):
    return lax.dot_general(
        left, right, (dims, ((), ())), precision=lax.Precision.HIGHEST, preferred_element_type=F32
    )


def squeeze_kernel(t_hbm, f3_hbm, f4t_hbm, f5_hbm, out_ref, t_ref, f3_ref, f4t_ref, f5_ref, main_h, main_l, rest, mix_h, mix_l, sems):
    small = [
        pltpu.make_async_copy(src, dst, sems.at[ROWS + n])
        for n, (src, dst) in enumerate(((f3_hbm, f3_ref), (f4t_hbm, f4t_ref), (f5_hbm, f5_ref)))
    ]
    loads = [pltpu.make_async_copy(t_hbm.at[i], t_ref.at[i], sems.at[i]) for i in range(ROWS)]
    for copy in small + loads:
        copy.start()
    for copy in small:
        copy.wait()

    lane = lax.broadcasted_iota(jnp.int32, (R4, PAIR), 1)
    row = lax.broadcasted_iota(jnp.int32, (R4, PAIR), 0)
    spread_four = (lane // R5 == row).astype(F32)
    lane = lax.broadcasted_iota(jnp.int32, (R5, PAIR), 1)
    row = lax.broadcasted_iota(jnp.int32, (R5, PAIR), 0)
    spread_five = (lane % R5 == row).astype(F32)
    four = exact_dot(f4t_ref[...], spread_four, ((0,), (0,)))
    five = exact_dot(f5_ref[...], spread_five, ((1,), (0,)))
    pair = (four[:, None, :] * five[None, :, :]).reshape(INNER, PAIR)
    high, low = split(pair)
    main_h[:, :PAIR] = high
    main_h[:, PAIR:] = low
    tail_h, tail_l = high[MAIN:], low[MAIN:]
    rest[...] = jnp.concatenate(
        [
            jnp.concatenate([tail_h, tail_l], axis=1),
            jnp.concatenate([tail_h, jnp.zeros_like(tail_l)], axis=1),
        ],
        axis=0,
    )
    size = R3 * DEPTH
    a_row = lax.broadcasted_iota(jnp.int32, (size, I3), 0) // DEPTH
    a_col = lax.broadcasted_iota(jnp.int32, (size, I3), 1)
    pick = (a_row == a_col).astype(F32)
    rows = exact_dot(pick, f3_ref[...], ((1,), (1,)))
    full = exact_dot(rows, pick, ((1,), (1,)))
    same = (
        lax.broadcasted_iota(jnp.int32, (size, size), 0) % DEPTH
        == lax.broadcasted_iota(jnp.int32, (size, size), 1) % DEPTH
    )
    high, low = split(jnp.where(same, full, 0.0))
    mix_h[...] = high
    mix_l[...] = low

    size_in = R3 * DEPTH
    peak = jnp.zeros((8, PAIR), F32)
    for base in range(0, ROWS, 7):
        group = range(base, base + 7)
        for i in group:
            loads[i].wait()
        halves = [split(t_ref[i]) for i in group]
        starts = [a * INNER for a in range(I3)]
        left_h = jnp.concatenate([h[:, s:s + INNER] for h, _ in halves for s in starts], axis=0)
        left_l = jnp.concatenate([l[:, s:s + INNER] for _, l in halves for s in starts], axis=0)
        both = dot(left_h, main_h[...])
        stack = both[:, :PAIR] + (both[:, PAIR:] + dot(left_l, main_h[:, :PAIR]))
        for n, i in enumerate(group):
            inner_h, inner_l = split(stack[n * size_in:(n + 1) * size_in])
            both = dot(mix_h[...], jnp.concatenate([inner_h, inner_l], axis=1))
            outer = both[:, :PAIR] + (both[:, PAIR:] + dot(mix_l[...], inner_h))
            out_ref[:, i * WIDE:(i + 1) * WIDE] = outer.reshape(NARROW, WIDE, PAIR)
            peak = jnp.maximum(peak, jnp.max(jnp.abs(outer).reshape(-1, 8, PAIR), axis=0))

    level = exponent(jnp.broadcast_to(jnp.max(peak, keepdims=True), (8, PAIR)))
    factor = jnp.exp2(-level)
    for n in range(NARROW):
        block = out_ref[n, :ROWS * WIDE].reshape(-1, 8, PAIR) * factor
        out_ref[n, :ROWS * WIDE] = block.reshape(ROWS * WIDE, PAIR)
        out_ref[n, ROWS * WIDE:] = level


def squeeze(tensor, f3, f4t, f5):
    size = R3 * DEPTH
    hbm = pl.BlockSpec(memory_space=pltpu.MemorySpace.HBM)
    return pl.pallas_call(
        squeeze_kernel,
        in_specs=[hbm] * 4,
        out_shape=jax.ShapeDtypeStruct((NARROW, ROWS * WIDE + 8, PAIR), F32),
        scratch_shapes=[
            pltpu.VMEM((ROWS, DEPTH, CELLS), F32),
            pltpu.VMEM((I3, R3), F32),
            pltpu.VMEM((R4, I4), F32),
            pltpu.VMEM((I5, R5), F32),
            pltpu.VMEM((INNER, 2 * PAIR), BF16),
            pltpu.VMEM((MAIN, PAIR), BF16),
            pltpu.VMEM((2 * (INNER - MAIN), 2 * PAIR), BF16),
            pltpu.VMEM((size, size), BF16),
            pltpu.VMEM((size, size), BF16),
            pltpu.SemaphoreType.DMA((ROWS + 3,)),
        ],
        compiler_params=pltpu.CompilerParams(vmem_limit_bytes=61 * 1024 * 1024),
    )(tensor, f3, f4t, f5)


def expand_kernel(x_ref, f2t_ref, out_ref, rows_ref):
    high, low = split(f2t_ref[...])
    left = jnp.concatenate([high, low], axis=0)
    factor = jnp.exp2(x_ref[:, ROWS * WIDE:])
    for i in range(ROWS):
        piece = x_ref[:, i * WIDE:(i + 1) * WIDE].reshape(NARROW, WIDE // 8, 8, PAIR) * factor[:, None]
        piece_h, piece_l = split(piece.reshape(NARROW, WIDE, PAIR))
        right_h, right_l = (
            jnp.concatenate(
                [p[:, h * DEPTH:(h + 1) * DEPTH].reshape(NARROW * DEPTH, PAIR) for h in range(2)], axis=1
            )
            for p in (piece_h, piece_l)
        )
        both = dot(left, right_h)
        core = both[:R2] + (both[R2:] + dot(high, right_l))
        for h in range(2):
            rows_ref[h, pl.ds(i, R2, stride=PAD), :] = core[:, h * PAIR:(h + 1) * PAIR]
    keep = lax.broadcasted_iota(jnp.int32, (R2, PAD, PAIR), 1) < ROWS
    for h in range(2):
        block = jnp.where(keep, rows_ref[h].reshape(R2, PAD, PAIR), 0.0)
        out_ref[:, :, :, h * PAIR:(h + 1) * PAIR] = block.astype(BF16).reshape(GROUPS, -1, PAD, PAIR)


def expand(gathered, f2t):
    return pl.pallas_call(
        expand_kernel,
        out_shape=jax.ShapeDtypeStruct((GROUPS, R2 // GROUPS, PAD, 2 * PAIR), BF16),
        scratch_shapes=[pltpu.VMEM((2, R2 * PAD, PAIR), F32)],
        compiler_params=pltpu.CompilerParams(vmem_limit_bytes=VMEM_LIMIT),
    )(gathered, f2t)


def gram_kernel(own_ref, other_ref, out_ref):
    total = None
    for q in range(R2 // GROUPS):
        left = own_ref[:, q].reshape(GROUPS * PAD, 2 * PAIR)
        right = jnp.concatenate(
            [ref[g, q] for g in range(GROUPS) for ref in (own_ref, other_ref)], axis=0
        )
        part = lax.dot_general(left, right, (((1,), (1,)), ((), ())), preferred_element_type=F32)
        total = part if total is None else total + part
    peak = jnp.max(jnp.abs(total), axis=0, keepdims=True)
    level = exponent(jnp.broadcast_to(jnp.max(peak, axis=1, keepdims=True), (8, 128)))
    total = total * jnp.exp2(-level[:1, :1])
    first = lax.broadcasted_iota(jnp.int32, (8, 128), 1) < 64
    last = lax.broadcasted_iota(jnp.int32, (8, 128), 0) == 7
    for g in range(GROUPS):
        for n in range(0, NARROW, 2):
            top = total[g * PAD:g * PAD + 8, n * 64:n * 64 + 128]
            bottom = jnp.where(last, level, total[g * PAD + 8:(g + 1) * PAD, n * 64:n * 64 + 128])
            out_ref[g * NARROW + n] = jnp.where(first, top, pltpu.roll(bottom, 64, 1))
            out_ref[g * NARROW + n + 1] = jnp.where(first, pltpu.roll(top, 64, 1), bottom)


def gram(own, other):
    return pl.pallas_call(
        gram_kernel,
        out_shape=jax.ShapeDtypeStruct((GROUPS * NARROW, 8, 128), F32),
        compiler_params=pltpu.CompilerParams(vmem_limit_bytes=VMEM_LIMIT),
    )(own, other)


def finish_kernel(x_ref, out_ref):
    scale = 1.0 / math.sqrt(R2 * R3 * R4 * R5)
    factor = jnp.exp2(x_ref[:, 7:8, 64:65])
    total = jnp.sum(x_ref[...] * factor, axis=0) * scale
    rows = jnp.concatenate([total[:, :64], total[:, 64:]], axis=0)[:ROWS]
    group = [rows[:, g * PAD:g * PAD + ROWS] for g in range(4)]
    first = lax.axis_index("core") == 0
    out_ref[...] = jnp.where(
        first, jnp.concatenate(group, axis=1), jnp.concatenate([group[g ^ 1] for g in range(4)], axis=1)
    )


def finish(parts):
    return pl.pallas_call(
        finish_kernel,
        out_shape=jax.ShapeDtypeStruct((ROWS, 4 * ROWS), F32),
        compiler_params=pltpu.CompilerParams(vmem_limit_bytes=VMEM_LIMIT),
    )(parts)


def exchange(value, axes):
    sent = lax.all_to_all(value.astype(F16), axes, 0, 0, tiled=True)
    return sent.astype(F32)


def per_device(tensor, f2, f3, f4, f5):
    with jax.named_scope("squeeze"):
        reduced = squeeze(tensor, f3, f4.T, f5)
    with jax.named_scope("depth_exchange"):
        gathered = exchange(reduced, ("x_hi", "y"))
    with jax.named_scope("expand"):
        core = expand(gathered, f2.T)
    with jax.named_scope("row_exchange"):
        rows = lax.all_to_all(core, ("z", "x_lo"), 0, 0, tiled=True)
    with jax.named_scope("core_swap"):
        other = lax.ppermute(rows, "core", [(0, 1), (1, 0)])
    with jax.named_scope("gram"):
        parts = gram(rows, other)
    with jax.named_scope("gram_exchange"):
        parts = exchange(parts, ("z", "x_lo", "x_hi", "y"))
    with jax.named_scope("finish"):
        return finish(parts)


def solution(mesh):
    fine = Mesh(
        mesh.devices.reshape(Z, XL, CORE, XH, Y), ("z", "x_lo", "core", "x_hi", "y")
    )
    blk, narrow = ("z", "x_lo", "core"), ("x_hi", "y")
    return jax.shard_map(
        per_device,
        mesh=fine,
        in_specs=(P(blk, narrow, None), P(), P(), P(), P()),
        out_specs=P(blk, narrow),
        check_vma=False,
    )
```

```python
import math

import jax
import jax.numpy as jnp
from jax import lax
from jax.experimental import pallas as pl
from jax.experimental.pallas import tpu as pltpu
from jax.sharding import Mesh, PartitionSpec as P

F32 = jnp.float32
BF16 = jnp.bfloat16
F16 = jnp.float16
ROWS, DEPTH, I3, I4, I5 = 14, 16, 16, 33, 8
R2, R3, R4, R5 = 64, 16, 16, 8
CELLS = I3 * I4 * I5
INNER = I4 * I5
PAIR = R4 * R5
WIDE = R3 * DEPTH // 8
PAD = 16
ROWS_STEP = 2
Z, XL, CORE, XH, Y = 8, 2, 2, 2, 4
NARROW = XH * Y
GROUPS = Z * XL
VMEM_LIMIT = 32 * 1024 * 1024


def split(value):
    high = value.astype(BF16)
    return high, (value - high.astype(F32)).astype(BF16)


def dot(left, right):
    return lax.dot_general(left, right, (((1,), (0,)), ((), ())), preferred_element_type=F32)


def exponent(peak, target):
    return jnp.floor(jnp.log2(jnp.maximum(peak, 1e-30))) - target


def encode(value):
    square = value * value
    fourth = square * square
    return (fourth * fourth * value).astype(BF16)


def decode(code, level):
    wide = code.astype(F32)
    size = jnp.exp2(jnp.log2(jnp.abs(wide)) * (1.0 / 9.0) + level)
    return jnp.where(wide == 0.0, 0.0, jnp.where(wide < 0.0, -size, size))


def exact_dot(left, right, dims):
    return lax.dot_general(
        left, right, (dims, ((), ())), precision=lax.Precision.HIGHEST, preferred_element_type=F32
    )


def squeeze_kernel(
    t_hbm, f3_hbm, f4t_hbm, f5_hbm, out_hbm,
    t_ref, f3_ref, f4t_ref, f5_ref, rows_ref, main_h, mix_h, mix_l, code_ref, sems, out_sems,
):
    small = [
        pltpu.make_async_copy(src, dst, sems.at[ROWS + n])
        for n, (src, dst) in enumerate(
            ((f3_hbm, f3_ref), (f4t_hbm, f4t_ref), (f5_hbm, f5_ref))
        )
    ]
    loads = [pltpu.make_async_copy(t_hbm.at[i], t_ref.at[i], sems.at[i]) for i in range(ROWS)]
    for copy in small + loads:
        copy.start()
    for copy in small:
        copy.wait()

    lane = lax.broadcasted_iota(jnp.int32, (R4, PAIR), 1)
    row = lax.broadcasted_iota(jnp.int32, (R4, PAIR), 0)
    spread_four = (lane // R5 == row).astype(F32)
    lane = lax.broadcasted_iota(jnp.int32, (R5, PAIR), 1)
    row = lax.broadcasted_iota(jnp.int32, (R5, PAIR), 0)
    spread_five = (lane % R5 == row).astype(F32)
    four = exact_dot(f4t_ref[...], spread_four, ((0,), (0,)))
    five = exact_dot(f5_ref[...], spread_five, ((1,), (0,)))
    pair = (four[:, None, :] * five[None, :, :]).reshape(INNER, PAIR)
    high, low = split(pair)
    main_h[:, :PAIR] = high
    main_h[:, PAIR:] = low
    size = R3 * DEPTH
    a_row = lax.broadcasted_iota(jnp.int32, (size, I3), 0) // DEPTH
    a_col = lax.broadcasted_iota(jnp.int32, (size, I3), 1)
    pick = (a_row == a_col).astype(F32)
    rows = exact_dot(pick, f3_ref[...], ((1,), (1,)))
    full = exact_dot(rows, pick, ((1,), (1,)))
    same = (
        lax.broadcasted_iota(jnp.int32, (size, size), 0) % DEPTH
        == lax.broadcasted_iota(jnp.int32, (size, size), 1) % DEPTH
    )
    high, low = split(jnp.where(same, full, 0.0))
    mix_h[...] = high
    mix_l[...] = low

    size_in = R3 * DEPTH
    peak = jnp.zeros((8, PAIR), F32)
    for base in range(0, ROWS, 7):
        group = range(base, base + 7)
        for i in group:
            loads[i].wait()
        halves = [split(t_ref[i]) for i in group]
        starts = [a * INNER for a in range(I3)]
        left_h = jnp.concatenate([h[:, s:s + INNER] for h, _ in halves for s in starts], axis=0)
        left_l = jnp.concatenate([l[:, s:s + INNER] for _, l in halves for s in starts], axis=0)
        both = dot(left_h, main_h[...])
        stack = both[:, :PAIR] + (both[:, PAIR:] + dot(left_l, main_h[:, :PAIR]))
        for n, i in enumerate(group):
            inner_h, inner_l = split(stack[n * size_in:(n + 1) * size_in])
            both = dot(mix_h[...], jnp.concatenate([inner_h, inner_l], axis=1))
            outer = both[:, :PAIR] + (both[:, PAIR:] + dot(mix_l[...], inner_h))
            rows_ref[:, i * WIDE:(i + 1) * WIDE] = outer.reshape(NARROW, WIDE, PAIR)
            peak = jnp.maximum(peak, jnp.max(jnp.abs(outer).reshape(-1, 8, PAIR), axis=0))

    level = exponent(jnp.broadcast_to(jnp.max(peak, keepdims=True), (8, PAIR)), 12.0)
    factor = jnp.exp2(-level)
    stores = []
    for n in range(NARROW):
        block = rows_ref[n].reshape(-1, 8, PAIR) * factor
        code_ref[n, :ROWS * WIDE] = encode(block).reshape(ROWS * WIDE, PAIR)
        code_ref[n, ROWS * WIDE:] = jnp.concatenate([level, level], axis=0).astype(BF16)
        stores.append(pltpu.make_async_copy(code_ref.at[n], out_hbm.at[n], out_sems.at[n]))
        stores[-1].start()
    for copy in stores:
        copy.wait()


def squeeze(tensor, f3, f4t, f5):
    size = R3 * DEPTH
    hbm = pl.BlockSpec(memory_space=pltpu.MemorySpace.HBM)
    return pl.pallas_call(
        squeeze_kernel,
        in_specs=[hbm] * 4,
        out_specs=hbm,
        out_shape=jax.ShapeDtypeStruct((NARROW, ROWS * WIDE + 16, PAIR), BF16),
        scratch_shapes=[
            pltpu.VMEM((ROWS, DEPTH, CELLS), F32),
            pltpu.VMEM((I3, R3), F32),
            pltpu.VMEM((R4, I4), F32),
            pltpu.VMEM((I5, R5), F32),
            pltpu.VMEM((NARROW, ROWS * WIDE, PAIR), F32),
            pltpu.VMEM((INNER, 2 * PAIR), BF16),
            pltpu.VMEM((size, size), BF16),
            pltpu.VMEM((size, size), BF16),
            pltpu.VMEM((NARROW, ROWS * WIDE + 16, PAIR), BF16),
            pltpu.SemaphoreType.DMA((ROWS + 3,)),
            pltpu.SemaphoreType.DMA((NARROW,)),
        ],
        compiler_params=pltpu.CompilerParams(vmem_limit_bytes=61 * 1024 * 1024),
    )(tensor, f3, f4t, f5)


def expand_kernel(x_ref, f2t_ref, out_ref, rows_ref):
    high, low = split(f2t_ref[...])
    left = jnp.concatenate([high, low], axis=0)
    level = x_ref[:, ROWS * WIDE:].astype(F32)[:, None]
    for i in range(ROWS):
        code = x_ref[:, i * WIDE:(i + 1) * WIDE].reshape(NARROW, WIDE // 16, 16, PAIR)
        piece_h, piece_l = split(decode(code, level).reshape(NARROW, WIDE, PAIR))
        right_h, right_l = (
            jnp.concatenate(
                [p[:, h * DEPTH:(h + 1) * DEPTH].reshape(NARROW * DEPTH, PAIR) for h in range(2)], axis=1
            )
            for p in (piece_h, piece_l)
        )
        both = dot(left, right_h)
        core = both[:R2] + (both[R2:] + dot(left[:R2], right_l))
        for h in range(2):
            rows_ref[h, pl.ds(i, R2, stride=PAD), :] = core[:, h * PAIR:(h + 1) * PAIR]
    keep = lax.broadcasted_iota(jnp.int32, (R2, PAD, PAIR), 1) < ROWS
    for h in range(2):
        block = jnp.where(keep, rows_ref[h].reshape(R2, PAD, PAIR), 0.0)
        out_ref[:, :, :, h * PAIR:(h + 1) * PAIR] = block.astype(BF16).reshape(GROUPS, -1, PAD, PAIR)


def expand(gathered, f2t):
    return pl.pallas_call(
        expand_kernel,
        out_shape=jax.ShapeDtypeStruct((GROUPS, R2 // GROUPS, PAD, 2 * PAIR), BF16),
        scratch_shapes=[pltpu.VMEM((2, R2 * PAD, PAIR), F32)],
        compiler_params=pltpu.CompilerParams(vmem_limit_bytes=VMEM_LIMIT),
    )(gathered, f2t)


def gram_kernel(own_ref, other_ref, out_ref):
    total = None
    for q in range(R2 // GROUPS):
        left = own_ref[:, q].reshape(GROUPS * PAD, 2 * PAIR)
        right = jnp.concatenate(
            [ref[g, q] for g in range(GROUPS) for ref in (own_ref, other_ref)], axis=0
        )
        part = lax.dot_general(left, right, (((1,), (1,)), ((), ())), preferred_element_type=F32)
        total = part if total is None else total + part
    peak = jnp.max(jnp.abs(total), axis=0, keepdims=True)
    level = exponent(jnp.broadcast_to(jnp.max(peak, axis=1, keepdims=True), (8, 128)), 14.0)
    total = total * jnp.exp2(-level[:1, :1])
    first = lax.broadcasted_iota(jnp.int32, (8, 128), 1) < 64
    last = lax.broadcasted_iota(jnp.int32, (8, 128), 0) == 7
    for g in range(GROUPS):
        for n in range(0, NARROW, 2):
            top = total[g * PAD:g * PAD + 8, n * 64:n * 64 + 128]
            bottom = jnp.where(last, level, total[g * PAD + 8:(g + 1) * PAD, n * 64:n * 64 + 128])
            out_ref[g * NARROW + n] = jnp.where(first, top, pltpu.roll(bottom, 64, 1))
            out_ref[g * NARROW + n + 1] = jnp.where(first, pltpu.roll(top, 64, 1), bottom)


def gram(own, other):
    return pl.pallas_call(
        gram_kernel,
        out_shape=jax.ShapeDtypeStruct((GROUPS * NARROW, 8, 128), F32),
        compiler_params=pltpu.CompilerParams(vmem_limit_bytes=VMEM_LIMIT),
    )(own, other)


def finish_kernel(x_ref, out_ref):
    scale = 1.0 / math.sqrt(R2 * R3 * R4 * R5)
    factor = jnp.exp2(x_ref[:, 7:8, 64:65])
    total = jnp.sum(x_ref[...] * factor, axis=0) * scale
    rows = jnp.concatenate([total[:, :64], total[:, 64:]], axis=0)[:ROWS]
    group = [rows[:, g * PAD:g * PAD + ROWS] for g in range(4)]
    first = lax.axis_index("core") == 0
    out_ref[...] = jnp.where(
        first, jnp.concatenate(group, axis=1), jnp.concatenate([group[g ^ 1] for g in range(4)], axis=1)
    )


def finish(parts):
    return pl.pallas_call(
        finish_kernel,
        out_shape=jax.ShapeDtypeStruct((ROWS, 4 * ROWS), F32),
        compiler_params=pltpu.CompilerParams(vmem_limit_bytes=VMEM_LIMIT),
    )(parts)


def per_device(tensor, f2, f3, f4, f5):
    with jax.named_scope("squeeze"):
        reduced = squeeze(tensor, f3, f4.T, f5)
    with jax.named_scope("depth_exchange"):
        gathered = lax.all_to_all(reduced, ("x_hi", "y"), 0, 0, tiled=True)
    with jax.named_scope("expand"):
        core = expand(gathered, f2.T)
    with jax.named_scope("row_exchange"):
        rows = lax.all_to_all(core, ("z", "x_lo"), 0, 0, tiled=True)
    with jax.named_scope("core_swap"):
        other = lax.ppermute(rows, "core", [(0, 1), (1, 0)])
    with jax.named_scope("gram"):
        parts = gram(rows, other)
    with jax.named_scope("gram_exchange"):
        parts = lax.all_to_all(parts.astype(F16), ("z", "x_lo", "x_hi", "y"), 0, 0, tiled=True).astype(F32)
    with jax.named_scope("finish"):
        return finish(parts)


def solution(mesh):
    fine = Mesh(
        mesh.devices.reshape(Z, XL, CORE, XH, Y), ("z", "x_lo", "core", "x_hi", "y")
    )
    blk, narrow = ("z", "x_lo", "core"), ("x_hi", "y")
    return jax.shard_map(
        per_device,
        mesh=fine,
        in_specs=(P(blk, narrow, None), P(), P(), P(), P()),
        out_specs=P(blk, narrow),
        check_vma=False,
    )
```

```python
import math

import jax
import jax.numpy as jnp
from jax import lax
from jax.experimental import pallas as pl
from jax.experimental.pallas import tpu as pltpu
from jax.sharding import Mesh, PartitionSpec as P

F32 = jnp.float32
BF16 = jnp.bfloat16
F16 = jnp.float16
ROWS, DEPTH, I3, I4, I5 = 14, 16, 16, 33, 8
R2, R3, R4, R5 = 64, 16, 16, 8
CELLS = I3 * I4 * I5
INNER = I4 * I5
PAIR = R4 * R5
WIDE = R3 * DEPTH // 8
PAD = 16
ROWS_STEP = 2
Z, XL, CORE, XH, Y = 8, 2, 2, 2, 4
NARROW = XH * Y
GROUPS = Z * XL
SLICES = R2 // GROUPS * 2
BLOCK = SLICES * ROWS
VMEM_LIMIT = 32 * 1024 * 1024


def split(value):
    high = value.astype(BF16)
    return high, (value - high.astype(F32)).astype(BF16)


def dot(left, right):
    return lax.dot_general(left, right, (((1,), (0,)), ((), ())), preferred_element_type=F32)


def exponent(peak, target):
    return jnp.floor(jnp.log2(jnp.maximum(peak, 1e-30))) - target


def encode(value):
    square = value * value
    fourth = square * square
    return (fourth * fourth * value).astype(BF16)


def decode(code, level):
    wide = code.astype(F32)
    size = jnp.exp2(jnp.log2(jnp.abs(wide)) * (1.0 / 9.0) + level)
    return jnp.where(wide == 0.0, 0.0, jnp.where(wide < 0.0, -size, size))


def exact_dot(left, right, dims):
    return lax.dot_general(
        left, right, (dims, ((), ())), precision=lax.Precision.HIGHEST, preferred_element_type=F32
    )


def squeeze_kernel(
    t_hbm, f3_hbm, f4t_hbm, f5_hbm, out_ref,
    t_ref, f3_ref, f4t_ref, f5_ref, rows_ref, main_h, mix_h, mix_l, sems,
):
    small = [
        pltpu.make_async_copy(src, dst, sems.at[ROWS + n])
        for n, (src, dst) in enumerate(
            ((f3_hbm, f3_ref), (f4t_hbm, f4t_ref), (f5_hbm, f5_ref))
        )
    ]
    loads = [pltpu.make_async_copy(t_hbm.at[i], t_ref.at[i], sems.at[i]) for i in range(ROWS)]
    for copy in small + loads:
        copy.start()
    for copy in small:
        copy.wait()

    lane = lax.broadcasted_iota(jnp.int32, (R4, PAIR), 1)
    row = lax.broadcasted_iota(jnp.int32, (R4, PAIR), 0)
    spread_four = (lane // R5 == row).astype(F32)
    lane = lax.broadcasted_iota(jnp.int32, (R5, PAIR), 1)
    row = lax.broadcasted_iota(jnp.int32, (R5, PAIR), 0)
    spread_five = (lane % R5 == row).astype(F32)
    four = exact_dot(f4t_ref[...], spread_four, ((0,), (0,)))
    five = exact_dot(f5_ref[...], spread_five, ((1,), (0,)))
    pair = (four[:, None, :] * five[None, :, :]).reshape(INNER, PAIR)
    high, low = split(pair)
    main_h[:, :PAIR] = high
    main_h[:, PAIR:] = low
    size = R3 * DEPTH
    a_row = lax.broadcasted_iota(jnp.int32, (size, I3), 0) // DEPTH
    a_col = lax.broadcasted_iota(jnp.int32, (size, I3), 1)
    pick = (a_row == a_col).astype(F32)
    rows = exact_dot(pick, f3_ref[...], ((1,), (1,)))
    full = exact_dot(rows, pick, ((1,), (1,)))
    same = (
        lax.broadcasted_iota(jnp.int32, (size, size), 0) % DEPTH
        == lax.broadcasted_iota(jnp.int32, (size, size), 1) % DEPTH
    )
    high, low = split(jnp.where(same, full, 0.0))
    mix_h[...] = high
    mix_l[...] = low

    size_in = R3 * DEPTH
    peak = jnp.zeros((8, PAIR), F32)
    for base in range(0, ROWS, 7):
        group = range(base, base + 7)
        for i in group:
            loads[i].wait()
        halves = [split(t_ref[i]) for i in group]
        starts = [a * INNER for a in range(I3)]
        left_h = jnp.concatenate([h[:, s:s + INNER] for h, _ in halves for s in starts], axis=0)
        left_l = jnp.concatenate([l[:, s:s + INNER] for _, l in halves for s in starts], axis=0)
        both = dot(left_h, main_h[...])
        stack = both[:, :PAIR] + (both[:, PAIR:] + dot(left_l, main_h[:, :PAIR]))
        for n, i in enumerate(group):
            inner_h, inner_l = split(stack[n * size_in:(n + 1) * size_in])
            both = dot(mix_h[...], jnp.concatenate([inner_h, inner_l], axis=1))
            outer = both[:, :PAIR] + (both[:, PAIR:] + dot(mix_l[...], inner_h))
            rows_ref[:, i * WIDE:(i + 1) * WIDE] = outer.reshape(NARROW, WIDE, PAIR)
            peak = jnp.maximum(peak, jnp.max(jnp.abs(outer).reshape(-1, 8, PAIR), axis=0))

    level = exponent(jnp.broadcast_to(jnp.max(peak, keepdims=True), (8, PAIR)), 12.0)
    factor = jnp.exp2(-level)
    for n in range(NARROW):
        block = rows_ref[n].reshape(-1, 8, PAIR) * factor
        out_ref[n, :ROWS * WIDE] = encode(block).reshape(ROWS * WIDE, PAIR)
        out_ref[n, ROWS * WIDE:] = jnp.concatenate([level, level], axis=0).astype(BF16)


def squeeze(tensor, f3, f4t, f5):
    size = R3 * DEPTH
    hbm = pl.BlockSpec(memory_space=pltpu.MemorySpace.HBM)
    return pl.pallas_call(
        squeeze_kernel,
        in_specs=[hbm] * 4,
        out_shape=pltpu.VMEM((NARROW, ROWS * WIDE + 16, PAIR), BF16),
        out_specs=pl.BlockSpec(memory_space=pltpu.VMEM),
        scratch_shapes=[
            pltpu.VMEM((ROWS, DEPTH, CELLS), F32),
            pltpu.VMEM((I3, R3), F32),
            pltpu.VMEM((R4, I4), F32),
            pltpu.VMEM((I5, R5), F32),
            pltpu.VMEM((NARROW, ROWS * WIDE, PAIR), F32),
            pltpu.VMEM((INNER, 2 * PAIR), BF16),
            pltpu.VMEM((size, size), BF16),
            pltpu.VMEM((size, size), BF16),
            pltpu.SemaphoreType.DMA((ROWS + 3,)),
        ],
        compiler_params=pltpu.CompilerParams(vmem_limit_bytes=58 * 1024 * 1024),
    )(tensor, f3, f4t, f5)


def expand_kernel(x_ref, f2t_ref, out_ref, rows_ref):
    high, low = split(f2t_ref[...])
    left = jnp.concatenate([high, low], axis=0)
    level = x_ref[:, ROWS * WIDE:].astype(F32)[:, None]
    for i in range(ROWS):
        code = x_ref[:, i * WIDE:(i + 1) * WIDE].reshape(NARROW, WIDE // 16, 16, PAIR)
        piece_h, piece_l = split(decode(code, level).reshape(NARROW, WIDE, PAIR))
        right_h, right_l = (
            jnp.concatenate(
                [p[:, h * DEPTH:(h + 1) * DEPTH].reshape(NARROW * DEPTH, PAIR) for h in range(2)], axis=1
            )
            for p in (piece_h, piece_l)
        )
        both = dot(left, right_h)
        core = both[:R2] + (both[R2:] + dot(left[:R2], right_l))
        for h in range(2):
            rows_ref[pl.ds(h * ROWS + i, R2, stride=2 * ROWS), :] = core[:, h * PAIR:(h + 1) * PAIR]
    out_ref[...] = rows_ref[...].astype(BF16).reshape(GROUPS, BLOCK, PAIR)


def expand(gathered, f2t):
    return pl.pallas_call(
        expand_kernel,
        out_shape=jax.ShapeDtypeStruct((GROUPS, BLOCK, PAIR), BF16),
        scratch_shapes=[pltpu.VMEM((R2 * 2 * ROWS, PAIR), F32)],
        compiler_params=pltpu.CompilerParams(vmem_limit_bytes=VMEM_LIMIT),
    )(gathered, f2t)


def gram_kernel(own_ref, other_ref, out_ref):
    row = lax.broadcasted_iota(jnp.int32, (SLICES * PAD, BLOCK), 0)
    col = lax.broadcasted_iota(jnp.int32, (SLICES * PAD, BLOCK), 1)
    spread = ((row % PAD < ROWS) & (row // PAD * ROWS + row % PAD == col)).astype(BF16)
    padded = [
        dot(spread, jnp.concatenate([own_ref[g], other_ref[g]], axis=1)).astype(BF16) for g in range(GROUPS)
    ]
    total = None
    for q in range(0, SLICES, 2):
        own, other = (
            [
                jnp.concatenate(
                    [both[p * PAD:(p + 1) * PAD, c * PAIR:(c + 1) * PAIR] for p in (q, q + 1)], axis=1
                )
                for both in padded
            ]
            for c in range(CORE)
        )
        left = jnp.concatenate(own, axis=0)
        right = jnp.concatenate([part for pair in zip(own, other) for part in pair], axis=0)
        part = lax.dot_general(left, right, (((1,), (1,)), ((), ())), preferred_element_type=F32)
        total = part if total is None else total + part
    peak = jnp.max(jnp.abs(total), axis=0, keepdims=True)
    level = exponent(jnp.broadcast_to(jnp.max(peak, axis=1, keepdims=True), (8, 128)), 14.0)
    total = total * jnp.exp2(-level[:1, :1])
    first = lax.broadcasted_iota(jnp.int32, (8, 128), 1) < 64
    last = lax.broadcasted_iota(jnp.int32, (8, 128), 0) == 7
    for g in range(GROUPS):
        for n in range(0, NARROW, 2):
            top = total[g * PAD:g * PAD + 8, n * 64:n * 64 + 128]
            bottom = jnp.where(last, level, total[g * PAD + 8:(g + 1) * PAD, n * 64:n * 64 + 128])
            out_ref[g * NARROW + n] = jnp.where(first, top, pltpu.roll(bottom, 64, 1))
            out_ref[g * NARROW + n + 1] = jnp.where(first, pltpu.roll(top, 64, 1), bottom)


def gram(own, other):
    return pl.pallas_call(
        gram_kernel,
        out_shape=jax.ShapeDtypeStruct((GROUPS * NARROW, 8, 128), F32),
        compiler_params=pltpu.CompilerParams(vmem_limit_bytes=VMEM_LIMIT),
    )(own, other)


def finish_kernel(x_ref, out_ref):
    scale = 1.0 / math.sqrt(R2 * R3 * R4 * R5)
    factor = jnp.exp2(x_ref[:, 7:8, 64:65])
    total = jnp.sum(x_ref[...] * factor, axis=0) * scale
    rows = jnp.concatenate([total[:, :64], total[:, 64:]], axis=0)[:ROWS]
    group = [rows[:, g * PAD:g * PAD + ROWS] for g in range(4)]
    first = lax.axis_index("core") == 0
    out_ref[...] = jnp.where(
        first, jnp.concatenate(group, axis=1), jnp.concatenate([group[g ^ 1] for g in range(4)], axis=1)
    )


def finish(parts):
    return pl.pallas_call(
        finish_kernel,
        out_shape=jax.ShapeDtypeStruct((ROWS, 4 * ROWS), F32),
        compiler_params=pltpu.CompilerParams(vmem_limit_bytes=VMEM_LIMIT),
    )(parts)


def per_device(tensor, f2, f3, f4, f5):
    with jax.named_scope("squeeze"):
        reduced = squeeze(tensor, f3, f4.T, f5)
    with jax.named_scope("depth_exchange"):
        gathered = lax.all_to_all(reduced, ("x_hi", "y"), 0, 0, tiled=True)
    with jax.named_scope("expand"):
        core = expand(gathered, f2.T)
    with jax.named_scope("row_exchange"):
        rows = lax.all_to_all(core, ("z", "x_lo"), 0, 0, tiled=True)
    with jax.named_scope("core_swap"):
        other = lax.ppermute(rows, "core", [(0, 1), (1, 0)])
    with jax.named_scope("gram"):
        parts = gram(rows, other)
    with jax.named_scope("gram_exchange"):
        parts = lax.all_to_all(parts.astype(F16), ("z", "x_lo", "x_hi", "y"), 0, 0, tiled=True).astype(F32)
    with jax.named_scope("finish"):
        return finish(parts)


def solution(mesh):
    fine = Mesh(
        mesh.devices.reshape(Z, XL, CORE, XH, Y), ("z", "x_lo", "core", "x_hi", "y")
    )
    blk, narrow = ("z", "x_lo", "core"), ("x_hi", "y")
    return jax.shard_map(
        per_device,
        mesh=fine,
        in_specs=(P(blk, narrow, None), P(), P(), P(), P()),
        out_specs=P(blk, narrow),
        check_vma=False,
    )
```

```python
import math

import jax
import jax.numpy as jnp
from jax import lax
from jax.experimental import pallas as pl
from jax.experimental.pallas import tpu as pltpu
from jax.sharding import Mesh, PartitionSpec as P

F32 = jnp.float32
BF16 = jnp.bfloat16
F16 = jnp.float16
ROWS, DEPTH, I3, I4, I5 = 14, 16, 16, 33, 8
R2, R3, R4, R5 = 64, 16, 16, 8
CELLS = I3 * I4 * I5
INNER = I4 * I5
PAIR = R4 * R5
WIDE = DEPTH
PAD = 16
SHIFT = 2.0 ** 24
ROWS_STEP = 2
Z, XL, CORE, XH, Y = 8, 2, 2, 2, 4
NARROW = XH * Y
FIRST = NARROW * XL
GROUPS = Z * XL
SLICES = R2 // Z * XL
BLOCK = SLICES * ROWS
VMEM_LIMIT = 32 * 1024 * 1024


def split(value):
    high = value.astype(BF16)
    return high, (value - high.astype(F32)).astype(BF16)


def dot(left, right):
    return lax.dot_general(left, right, (((1,), (0,)), ((), ())), preferred_element_type=F32)


def exponent(peak):
    return jnp.floor(jnp.log2(jnp.maximum(peak, 1e-30))) - 14.0


def encode(value):
    wide = value * SHIFT
    return (wide * wide * wide).astype(BF16)


def decode(code):
    wide = code.astype(F32)
    size = jnp.exp2(jnp.log2(jnp.abs(wide)) * (1.0 / 3.0)) * (1.0 / SHIFT)
    return jnp.where(wide == 0.0, 0.0, jnp.where(wide < 0.0, -size, size))


def exact_dot(left, right, dims):
    return lax.dot_general(
        left, right, (dims, ((), ())), precision=lax.Precision.HIGHEST, preferred_element_type=F32
    )


def squeeze_kernel(
    t_hbm, f3_hbm, f4t_hbm, f5_hbm, out_ref,
    t_ref, f3_ref, f4t_ref, f5_ref, main_h, mix_h, mix_l, sems,
):
    small = [
        pltpu.make_async_copy(src, dst, sems.at[ROWS + n])
        for n, (src, dst) in enumerate(
            ((f3_hbm, f3_ref), (f4t_hbm, f4t_ref), (f5_hbm, f5_ref))
        )
    ]
    loads = [pltpu.make_async_copy(t_hbm.at[i], t_ref.at[i], sems.at[i]) for i in range(ROWS)]
    for copy in small + loads:
        copy.start()
    for copy in small:
        copy.wait()

    lane = lax.broadcasted_iota(jnp.int32, (R4, PAIR), 1)
    row = lax.broadcasted_iota(jnp.int32, (R4, PAIR), 0)
    spread_four = (lane // R5 == row).astype(F32)
    lane = lax.broadcasted_iota(jnp.int32, (R5, PAIR), 1)
    row = lax.broadcasted_iota(jnp.int32, (R5, PAIR), 0)
    spread_five = (lane % R5 == row).astype(F32)
    four = exact_dot(f4t_ref[...], spread_four, ((0,), (0,)))
    five = exact_dot(f5_ref[...], spread_five, ((1,), (0,)))
    pair = (four[:, None, :] * five[None, :, :]).reshape(INNER, PAIR)
    high, low = split(pair)
    main_h[:, :PAIR] = high
    main_h[:, PAIR:] = low
    size = R3 * DEPTH
    a_row = lax.broadcasted_iota(jnp.int32, (size, I3), 0) // DEPTH
    a_col = lax.broadcasted_iota(jnp.int32, (size, I3), 1)
    pick = (a_row == a_col).astype(F32)
    rows = exact_dot(pick, f3_ref[...], ((1,), (1,)))
    full = exact_dot(rows, pick, ((1,), (1,)))
    same = (
        lax.broadcasted_iota(jnp.int32, (size, size), 0) % DEPTH
        == lax.broadcasted_iota(jnp.int32, (size, size), 1) % DEPTH
    )
    high, low = split(jnp.where(same, full, 0.0))
    mix_h[...] = high
    mix_l[...] = low

    size_in = R3 * DEPTH
    for base in range(0, ROWS, 7):
        group = range(base, base + 7)
        for i in group:
            loads[i].wait()
        halves = [split(t_ref[i]) for i in group]
        starts = [a * INNER for a in range(I3)]
        left_h = jnp.concatenate([h[:, s:s + INNER] for h, _ in halves for s in starts], axis=0)
        left_l = jnp.concatenate([l[:, s:s + INNER] for _, l in halves for s in starts], axis=0)
        both = dot(left_h, main_h[...])
        stack = both[:, :PAIR] + (both[:, PAIR:] + dot(left_l, main_h[:, :PAIR]))
        for n, i in enumerate(group):
            inner_h, inner_l = split(stack[n * size_in:(n + 1) * size_in])
            both = dot(mix_h[...], jnp.concatenate([inner_h, inner_l], axis=1))
            outer = both[:, :PAIR] + (both[:, PAIR:] + dot(mix_l[...], inner_h))
            out_ref[:, i * WIDE:(i + 1) * WIDE] = encode(outer).reshape(FIRST, WIDE, PAIR)


def squeeze(tensor, f3, f4t, f5):
    size = R3 * DEPTH
    hbm = pl.BlockSpec(memory_space=pltpu.MemorySpace.HBM)
    return pl.pallas_call(
        squeeze_kernel,
        in_specs=[hbm] * 4,
        out_shape=pltpu.VMEM((FIRST, ROWS * WIDE, PAIR), BF16),
        out_specs=pl.BlockSpec(memory_space=pltpu.VMEM),
        scratch_shapes=[
            pltpu.VMEM((ROWS, DEPTH, CELLS), F32),
            pltpu.VMEM((I3, R3), F32),
            pltpu.VMEM((R4, I4), F32),
            pltpu.VMEM((I5, R5), F32),
            pltpu.VMEM((INNER, 2 * PAIR), BF16),
            pltpu.VMEM((size, size), BF16),
            pltpu.VMEM((size, size), BF16),
            pltpu.SemaphoreType.DMA((ROWS + 3,)),
        ],
        compiler_params=pltpu.CompilerParams(vmem_limit_bytes=58 * 1024 * 1024),
    )(tensor, f3, f4t, f5)


def expand_kernel(x_ref, f2t_ref, out_ref, rows_ref):
    high, low = split(f2t_ref[...])
    left = jnp.concatenate([high, low], axis=0)
    for i in range(ROWS):
        code = x_ref[:, i * WIDE:(i + 1) * WIDE]
        pieces = split(decode(code).reshape(NARROW, XL, DEPTH, PAIR))
        right_h, right_l = (
            jnp.concatenate([p[:, x].reshape(NARROW * DEPTH, PAIR) for x in range(XL)], axis=1)
            for p in pieces
        )
        both = dot(left, right_h)
        core = both[:R2] + (both[R2:] + dot(left[:R2], right_l))
        for h in range(2):
            rows_ref[pl.ds(h * ROWS + i, R2, stride=2 * ROWS), :] = core[:, h * PAIR:(h + 1) * PAIR]
    out_ref[...] = rows_ref[...].astype(BF16).reshape(Z, BLOCK, PAIR)


def expand(gathered, f2t):
    return pl.pallas_call(
        expand_kernel,
        out_shape=jax.ShapeDtypeStruct((Z, BLOCK, PAIR), BF16),
        scratch_shapes=[pltpu.VMEM((R2 * 2 * ROWS, PAIR), F32)],
        compiler_params=pltpu.CompilerParams(vmem_limit_bytes=VMEM_LIMIT),
    )(gathered, f2t)


def gram_kernel(own_ref, other_ref, out_ref):
    row = lax.broadcasted_iota(jnp.int32, (SLICES * PAD, BLOCK), 0)
    col = lax.broadcasted_iota(jnp.int32, (SLICES * PAD, BLOCK), 1)
    spread = ((row % PAD < ROWS) & (row // PAD * ROWS + row % PAD == col)).astype(BF16)
    padded = [
        dot(spread, jnp.concatenate([own_ref[g], other_ref[g]], axis=1)).astype(BF16) for g in range(Z)
    ]
    total = None
    for q in range(0, SLICES, 2 * XL):
        own, other = (
            [
                jnp.concatenate(
                    [both[p * PAD:(p + 1) * PAD, c * PAIR:(c + 1) * PAIR] for p in (q + x, q + x + XL)], axis=1
                )
                for both in padded
                for x in range(XL)
            ]
            for c in range(CORE)
        )
        left = jnp.concatenate(own, axis=0)
        right = jnp.concatenate([part for pair in zip(own, other) for part in pair], axis=0)
        part = lax.dot_general(left, right, (((1,), (1,)), ((), ())), preferred_element_type=F32)
        total = part if total is None else total + part
    peak = jnp.max(jnp.abs(total), axis=0, keepdims=True)
    level = exponent(jnp.broadcast_to(jnp.max(peak, axis=1, keepdims=True), (8, 128)))
    total = total * jnp.exp2(-level[:1, :1])
    first = lax.broadcasted_iota(jnp.int32, (8, 128), 1) < 64
    last = lax.broadcasted_iota(jnp.int32, (8, 128), 0) == 7
    for g in range(GROUPS):
        for n in range(0, NARROW, 2):
            top = total[g * PAD:g * PAD + 8, n * 64:n * 64 + 128]
            bottom = jnp.where(last, level, total[g * PAD + 8:(g + 1) * PAD, n * 64:n * 64 + 128])
            out_ref[g * NARROW + n] = jnp.where(first, top, pltpu.roll(bottom, 64, 1))
            out_ref[g * NARROW + n + 1] = jnp.where(first, pltpu.roll(top, 64, 1), bottom)


def gram(own, other):
    return pl.pallas_call(
        gram_kernel,
        out_shape=jax.ShapeDtypeStruct((GROUPS * NARROW, 8, 128), F32),
        compiler_params=pltpu.CompilerParams(vmem_limit_bytes=VMEM_LIMIT),
    )(own, other)


def finish_kernel(x_ref, out_ref):
    scale = 1.0 / math.sqrt(R2 * R3 * R4 * R5)
    factor = jnp.exp2(x_ref[:, 7:8, 64:65])
    total = jnp.sum(x_ref[...] * factor, axis=0) * scale
    rows = jnp.concatenate([total[:, :64], total[:, 64:]], axis=0)[:ROWS]
    group = [rows[:, g * PAD:g * PAD + ROWS] for g in range(4)]
    first = lax.axis_index("core") == 0
    out_ref[...] = jnp.where(
        first, jnp.concatenate(group, axis=1), jnp.concatenate([group[g ^ 1] for g in range(4)], axis=1)
    )


def finish(parts):
    return pl.pallas_call(
        finish_kernel,
        out_shape=jax.ShapeDtypeStruct((ROWS, 4 * ROWS), F32),
        compiler_params=pltpu.CompilerParams(vmem_limit_bytes=VMEM_LIMIT),
    )(parts)


def per_device(tensor, f2, f3, f4, f5):
    with jax.named_scope("squeeze"):
        reduced = squeeze(tensor, f3, f4.T, f5)
    with jax.named_scope("depth_exchange"):
        gathered = lax.all_to_all(reduced, ("x_hi", "y", "x_lo"), 0, 0, tiled=True)
    with jax.named_scope("expand"):
        core = expand(gathered, f2.T)
    with jax.named_scope("row_exchange"):
        rows = lax.all_to_all(core, "z", 0, 0, tiled=True)
    with jax.named_scope("core_swap"):
        other = lax.ppermute(rows, "core", [(0, 1), (1, 0)])
    with jax.named_scope("gram"):
        parts = gram(rows, other)
    with jax.named_scope("gram_exchange"):
        parts = lax.all_to_all(parts.astype(F16), ("z", "x_lo", "x_hi", "y"), 0, 0, tiled=True).astype(F32)
    with jax.named_scope("finish"):
        return finish(parts)


def solution(mesh):
    fine = Mesh(
        mesh.devices.reshape(Z, XL, CORE, XH, Y), ("z", "x_lo", "core", "x_hi", "y")
    )
    blk, narrow = ("z", "x_lo", "core"), ("x_hi", "y")
    return jax.shard_map(
        per_device,
        mesh=fine,
        in_specs=(P(blk, narrow, None), P(), P(), P(), P()),
        out_specs=P(blk, narrow),
        check_vma=False,
    )
```

```python
import math

import jax
import jax.numpy as jnp
from jax import lax
from jax.experimental import pallas as pl
from jax.experimental.pallas import tpu as pltpu
from jax.sharding import Mesh, PartitionSpec as P

F32 = jnp.float32
BF16 = jnp.bfloat16
F16 = jnp.float16
ROWS, DEPTH, I3, I4, I5 = 14, 16, 16, 33, 8
R2, R3, R4, R5 = 64, 16, 16, 8
CELLS = I3 * I4 * I5
INNER = I4 * I5
PAIR = R4 * R5
WIDE = DEPTH
PAD = 16
SHIFT = 2.0 ** 24
ROWS_STEP = 2
Z, XL, CORE, XH, Y = 8, 2, 2, 2, 4
NARROW = XH * Y
FIRST = NARROW * XL
GROUPS = Z * XL
SLICES = R2 // Z * XL
BLOCK = SLICES * ROWS
VMEM_LIMIT = 32 * 1024 * 1024


def split(value):
    high = value.astype(BF16)
    return high, (value - high.astype(F32)).astype(BF16)


def dot(left, right):
    return lax.dot_general(left, right, (((1,), (0,)), ((), ())), preferred_element_type=F32)


def exponent(peak):
    return jnp.floor(jnp.log2(jnp.maximum(peak, 1e-30))) - 14.0


def encode(value):
    wide = value * SHIFT
    return (wide * wide * wide).astype(BF16)


def decode(code):
    wide = code.astype(F32)
    size = jnp.exp2(jnp.log2(jnp.abs(wide)) * (1.0 / 3.0)) * (1.0 / SHIFT)
    return jnp.where(wide == 0.0, 0.0, jnp.where(wide < 0.0, -size, size))


def exact_dot(left, right, dims):
    return lax.dot_general(
        left, right, (dims, ((), ())), precision=lax.Precision.HIGHEST, preferred_element_type=F32
    )


def squeeze_kernel(
    t_hbm, f3_hbm, f4t_hbm, f5_hbm, out_ref,
    t_ref, f3_ref, f4t_ref, f5_ref, main_h, mix_h, mix_l, sems,
):
    small = [
        pltpu.make_async_copy(src, dst, sems.at[ROWS + n])
        for n, (src, dst) in enumerate(
            ((f3_hbm, f3_ref), (f4t_hbm, f4t_ref), (f5_hbm, f5_ref))
        )
    ]
    loads = [pltpu.make_async_copy(t_hbm.at[i], t_ref.at[i], sems.at[i]) for i in range(ROWS)]
    for copy in small + loads:
        copy.start()
    for copy in small:
        copy.wait()

    lane = lax.broadcasted_iota(jnp.int32, (R4, PAIR), 1)
    row = lax.broadcasted_iota(jnp.int32, (R4, PAIR), 0)
    spread_four = (lane // R5 == row).astype(F32)
    lane = lax.broadcasted_iota(jnp.int32, (R5, PAIR), 1)
    row = lax.broadcasted_iota(jnp.int32, (R5, PAIR), 0)
    spread_five = (lane % R5 == row).astype(F32)
    four = exact_dot(f4t_ref[...], spread_four, ((0,), (0,)))
    five = exact_dot(f5_ref[...], spread_five, ((1,), (0,)))
    pair = (four[:, None, :] * five[None, :, :]).reshape(INNER, PAIR)
    high, low = split(pair)
    main_h[:, :PAIR] = high
    main_h[:, PAIR:] = low
    size = R3 * DEPTH
    a_row = lax.broadcasted_iota(jnp.int32, (size, I3), 0) // DEPTH
    a_col = lax.broadcasted_iota(jnp.int32, (size, I3), 1)
    pick = (a_row == a_col).astype(F32)
    rows = exact_dot(pick, f3_ref[...], ((1,), (1,)))
    full = exact_dot(rows, pick, ((1,), (1,)))
    same = (
        lax.broadcasted_iota(jnp.int32, (size, size), 0) % DEPTH
        == lax.broadcasted_iota(jnp.int32, (size, size), 1) % DEPTH
    )
    high, low = split(jnp.where(same, full, 0.0))
    mix_h[...] = high
    mix_l[...] = low

    size_in = R3 * DEPTH
    for base in range(0, ROWS, 7):
        group = range(base, base + 7)
        for i in group:
            loads[i].wait()
        halves = [split(t_ref[i]) for i in group]
        starts = [a * INNER for a in range(I3)]
        left_h = jnp.concatenate([h[:, s:s + INNER] for h, _ in halves for s in starts], axis=0)
        left_l = jnp.concatenate([l[:, s:s + INNER] for _, l in halves for s in starts], axis=0)
        both = dot(left_h, main_h[...])
        stack = both[:, :PAIR] + (both[:, PAIR:] + dot(left_l, main_h[:, :PAIR]))
        for n, i in enumerate(group):
            inner_h, inner_l = split(stack[n * size_in:(n + 1) * size_in])
            both = dot(mix_h[...], jnp.concatenate([inner_h, inner_l], axis=1))
            outer = both[:, :PAIR] + (both[:, PAIR:] + dot(mix_l[...], inner_h))
            out_ref[:, i * WIDE:(i + 1) * WIDE] = encode(outer).reshape(FIRST, WIDE, PAIR)


def squeeze(tensor, f3, f4t, f5):
    size = R3 * DEPTH
    hbm = pl.BlockSpec(memory_space=pltpu.MemorySpace.HBM)
    return pl.pallas_call(
        squeeze_kernel,
        in_specs=[hbm] * 4,
        out_shape=pltpu.VMEM((FIRST, ROWS * WIDE, PAIR), BF16),
        out_specs=pl.BlockSpec(memory_space=pltpu.VMEM),
        scratch_shapes=[
            pltpu.VMEM((ROWS, DEPTH, CELLS), F32),
            pltpu.VMEM((I3, R3), F32),
            pltpu.VMEM((R4, I4), F32),
            pltpu.VMEM((I5, R5), F32),
            pltpu.VMEM((INNER, 2 * PAIR), BF16),
            pltpu.VMEM((size, size), BF16),
            pltpu.VMEM((size, size), BF16),
            pltpu.SemaphoreType.DMA((ROWS + 3,)),
        ],
        compiler_params=pltpu.CompilerParams(vmem_limit_bytes=58 * 1024 * 1024),
    )(tensor, f3, f4t, f5)


def expand_kernel(x_ref, f2t_ref, out_ref, rows_ref):
    high, low = split(f2t_ref[...])
    left = jnp.concatenate([high, low], axis=0)
    for i in range(ROWS):
        code = x_ref[:, i * WIDE:(i + 1) * WIDE]
        pieces = split(decode(code).reshape(NARROW, XL, DEPTH, PAIR))
        right_h, right_l = (
            jnp.concatenate([p[:, x].reshape(NARROW * DEPTH, PAIR) for x in range(XL)], axis=1)
            for p in pieces
        )
        both = dot(left, right_h)
        core = both[:R2] + (both[R2:] + dot(left[:R2], right_l))
        for h in range(2):
            rows_ref[pl.ds(h * ROWS + i, R2, stride=2 * ROWS), :] = core[:, h * PAIR:(h + 1) * PAIR]
    out_ref[...] = rows_ref[...].astype(BF16).reshape(Z, BLOCK, PAIR)


def expand(gathered, f2t):
    return pl.pallas_call(
        expand_kernel,
        out_shape=jax.ShapeDtypeStruct((Z, BLOCK, PAIR), BF16),
        scratch_shapes=[pltpu.VMEM((R2 * 2 * ROWS, PAIR), F32)],
        compiler_params=pltpu.CompilerParams(vmem_limit_bytes=VMEM_LIMIT),
    )(gathered, f2t)


STEPS = R2 // Z // 2


def spread_rows(ref):
    row = lax.broadcasted_iota(jnp.int32, (SLICES * PAD, BLOCK), 0)
    col = lax.broadcasted_iota(jnp.int32, (SLICES * PAD, BLOCK), 1)
    spread = ((row % PAD < ROWS) & (row // PAD * ROWS + row % PAD == col)).astype(BF16)
    wide = [
        dot(spread, jnp.concatenate([ref[g], ref[g + 1]], axis=1)).astype(BF16) for g in range(0, Z, 2)
    ]
    padded = [both[:, h * PAIR:(h + 1) * PAIR] for both in wide for h in range(2)]
    span = XL * PAD
    return [
        jnp.concatenate(
            [
                jnp.concatenate([p[(2 * q + h) * span:(2 * q + h + 1) * span] for h in range(2)], axis=1)
                for p in padded
            ],
            axis=0,
        )
        for q in range(STEPS)
    ]


def outer_product(left, right):
    return lax.dot_general(left, right, (((1,), (1,)), ((), ())), preferred_element_type=F32)


def own_kernel(own_ref, left_ref, total_ref):
    rows = spread_rows(own_ref)
    for q in range(STEPS):
        left_ref[q] = rows[q]
    total_ref[...] = sum(outer_product(part, part) for part in rows)


def own_gram(own):
    size = GROUPS * PAD
    return pl.pallas_call(
        own_kernel,
        out_shape=(
            jax.ShapeDtypeStruct((STEPS, size, 2 * PAIR), BF16),
            jax.ShapeDtypeStruct((size, size), F32),
        ),
        cost_estimate=pl.CostEstimate(flops=400_000_000, bytes_accessed=1_200_000, transcendentals=0),
        compiler_params=pltpu.CompilerParams(vmem_limit_bytes=VMEM_LIMIT),
    )(own)


def gram_kernel(left_ref, own_ref, other_ref, out_ref):
    rows = spread_rows(other_ref)
    other = sum(outer_product(left_ref[q], rows[q]) for q in range(STEPS))
    own = own_ref[...]
    peak = jnp.max(jnp.maximum(jnp.abs(own), jnp.abs(other)), axis=0, keepdims=True)
    level = exponent(jnp.broadcast_to(jnp.max(peak, axis=1, keepdims=True), (8, 128)))
    factor = jnp.exp2(-level)
    lane = lax.broadcasted_iota(jnp.int32, (8, 128), 1)
    slot, mark = lane // 32, lane == PAD - 1
    for g in range(GROUPS):
        for tile in range(2):
            cols = slice(tile * 128, tile * 128 + 128)
            top, bottom = slice(g * PAD, g * PAD + 8), slice(g * PAD + 8, (g + 1) * PAD)
            parts = [
                own[top, cols] * factor,
                pltpu.roll(other[top, cols] * factor, 32, 1),
                pltpu.roll(own[bottom, cols] * factor, 64, 1),
                pltpu.roll(other[bottom, cols] * factor, 96, 1),
            ]
            for n in range(4):
                block = parts[0]
                for k in range(1, 4):
                    block = jnp.where(slot == (n + k) % 4, parts[k], block)
                out_ref[g * NARROW + tile * 4 + n] = jnp.where(mark, level, block)


def gram(left, own, other):
    return pl.pallas_call(
        gram_kernel,
        out_shape=jax.ShapeDtypeStruct((GROUPS * NARROW, 8, 128), F32),
        compiler_params=pltpu.CompilerParams(vmem_limit_bytes=VMEM_LIMIT),
    )(left, own, other)


def finish_kernel(x_ref, out_ref):
    scale = 1.0 / math.sqrt(R2 * R3 * R4 * R5)
    factor = jnp.exp2(x_ref[:, :, PAD - 1:PAD])
    total = jnp.sum(x_ref[...] * factor, axis=0) * scale
    place = lax.axis_index("y")
    turned = total
    for k in range(1, 4):
        turned = jnp.where(place == k, pltpu.roll(total, 128 - 32 * k, 1), turned)
    own = jnp.concatenate([turned[:, :32], turned[:, 64:96]], axis=0)[:ROWS]
    other = jnp.concatenate([turned[:, 32:64], turned[:, 96:]], axis=0)[:ROWS]
    group = [half[:, x * PAD:x * PAD + ROWS] for x in range(XL) for half in (own, other)]
    first = lax.axis_index("core") == 0
    out_ref[...] = jnp.where(
        first, jnp.concatenate(group, axis=1), jnp.concatenate([group[g ^ 1] for g in range(4)], axis=1)
    )


def finish(parts):
    return pl.pallas_call(
        finish_kernel,
        out_shape=jax.ShapeDtypeStruct((ROWS, 4 * ROWS), F32),
        compiler_params=pltpu.CompilerParams(vmem_limit_bytes=VMEM_LIMIT),
    )(parts)


def per_device(tensor, f2, f3, f4, f5):
    with jax.named_scope("squeeze"):
        reduced = squeeze(tensor, f3, f4.T, f5)
    with jax.named_scope("depth_exchange"):
        gathered = lax.all_to_all(reduced, ("x_hi", "y", "x_lo"), 0, 0, tiled=True)
    with jax.named_scope("expand"):
        core = expand(gathered, f2.T)
    with jax.named_scope("row_exchange"):
        rows = lax.all_to_all(core, "z", 0, 0, tiled=True)
    with jax.named_scope("core_swap"):
        other = lax.ppermute(rows, "core", [(0, 1), (1, 0)])
    with jax.named_scope("own_gram"):
        left, own = own_gram(rows)
    with jax.named_scope("gram"):
        parts = gram(left, own, other)
    with jax.named_scope("gram_exchange"):
        parts = lax.all_to_all(parts.astype(F16), ("z", "x_lo", "x_hi", "y"), 0, 0, tiled=True).astype(F32)
    with jax.named_scope("finish"):
        return finish(parts)


def solution(mesh):
    fine = Mesh(
        mesh.devices.reshape(Z, XL, CORE, XH, Y), ("z", "x_lo", "core", "x_hi", "y")
    )
    blk, narrow = ("z", "x_lo", "core"), ("x_hi", "y")
    return jax.shard_map(
        per_device,
        mesh=fine,
        in_specs=(P(blk, narrow, None), P(), P(), P(), P()),
        out_specs=P(blk, narrow),
        check_vma=False,
    )
```

```python
import math

import jax
import jax.numpy as jnp
from jax import lax
from jax.experimental import pallas as pl
from jax.experimental.pallas import tpu as pltpu
from jax.sharding import Mesh, PartitionSpec as P

F32 = jnp.float32
BF16 = jnp.bfloat16
F16 = jnp.float16
ROWS, DEPTH, I3, I4, I5 = 14, 16, 16, 33, 8
R2, R3, R4, R5 = 64, 16, 16, 8
CELLS = I3 * I4 * I5
INNER = I4 * I5
PAIR = R4 * R5
WIDE = DEPTH
PAD = 16
MAIN = 256
DEEP = 2 * INNER - MAIN
SHIFT_BITS = 24.0
SHIFT = 2.0 ** SHIFT_BITS
ROWS_STEP = 2
Z, XL, CORE, XH, Y = 8, 2, 2, 2, 4
NARROW = XH * Y
FIRST = NARROW * XL
GROUPS = Z * XL
SLICES = R2 // Z * XL
BLOCK = SLICES * ROWS
VMEM_LIMIT = 32 * 1024 * 1024


def split(value):
    high = value.astype(BF16)
    return high, (value - high.astype(F32)).astype(BF16)


def dot(left, right):
    return lax.dot_general(left, right, (((1,), (0,)), ((), ())), preferred_element_type=F32)


def exponent(peak):
    return jnp.floor(jnp.log2(jnp.maximum(peak, 1e-30))) - 14.0


def encode(value):
    wide = value * SHIFT
    return (wide * wide * wide).astype(BF16)


def decode(code):
    wide = code.astype(F32)
    power = jnp.log2(jnp.maximum(jnp.abs(wide), 1e-38))
    return wide * jnp.exp2(power * (-2.0 / 3.0) - SHIFT_BITS)


def exact_dot(left, right, dims):
    return lax.dot_general(
        left, right, (dims, ((), ())), precision=lax.Precision.HIGHEST, preferred_element_type=F32
    )


def squeeze_kernel(
    t_hbm, f3_hbm, f4t_hbm, f5_hbm, out_ref,
    t_ref, f3_ref, f4t_ref, f5_ref, main_h, mix_h, mix_l, sems,
):
    small = [
        pltpu.make_async_copy(src, dst, sems.at[ROWS + n])
        for n, (src, dst) in enumerate(
            ((f3_hbm, f3_ref), (f4t_hbm, f4t_ref), (f5_hbm, f5_ref))
        )
    ]
    loads = [pltpu.make_async_copy(t_hbm.at[i], t_ref.at[i], sems.at[i]) for i in range(ROWS)]
    for copy in small + loads:
        copy.start()
    for copy in small:
        copy.wait()

    lane = lax.broadcasted_iota(jnp.int32, (R4, PAIR), 1)
    row = lax.broadcasted_iota(jnp.int32, (R4, PAIR), 0)
    spread_four = (lane // R5 == row).astype(F32)
    lane = lax.broadcasted_iota(jnp.int32, (R5, PAIR), 1)
    row = lax.broadcasted_iota(jnp.int32, (R5, PAIR), 0)
    spread_five = (lane % R5 == row).astype(F32)
    four = exact_dot(f4t_ref[...], spread_four, ((0,), (0,)))
    five = exact_dot(f5_ref[...], spread_five, ((1,), (0,)))
    pair = (four[:, None, :] * five[None, :, :]).reshape(INNER, PAIR)
    high, low = split(pair)
    high, low = high.astype(F32), low.astype(F32)
    main_h[:, :PAIR] = jnp.concatenate([high, high[MAIN:]], axis=0).astype(BF16)
    main_h[:, PAIR:] = jnp.concatenate([low, jnp.zeros_like(low[MAIN:])], axis=0).astype(BF16)
    size = R3 * DEPTH
    a_row = lax.broadcasted_iota(jnp.int32, (size, I3), 0) // DEPTH
    a_col = lax.broadcasted_iota(jnp.int32, (size, I3), 1)
    pick = (a_row == a_col).astype(F32)
    rows = exact_dot(pick, f3_ref[...], ((1,), (1,)))
    full = exact_dot(rows, pick, ((1,), (1,)))
    same = (
        lax.broadcasted_iota(jnp.int32, (size, size), 0) % DEPTH
        == lax.broadcasted_iota(jnp.int32, (size, size), 1) % DEPTH
    )
    high, low = split(jnp.where(same, full, 0.0))
    mix_h[...] = high
    mix_l[...] = low

    size_in = R3 * DEPTH
    for base in range(0, ROWS, 7):
        group = range(base, base + 7)
        for i in group:
            loads[i].wait()
        halves = [split(t_ref[i]) for i in group]
        starts = [a * INNER for a in range(I3)]
        left_h = jnp.concatenate(
            [
                jnp.concatenate([h[:, s:s + INNER], l[:, s + MAIN:s + INNER]], axis=1)
                for h, l in halves
                for s in starts
            ],
            axis=0,
        )
        left_l = jnp.concatenate([l[:, s:s + MAIN] for _, l in halves for s in starts], axis=0)
        both = dot(left_h, main_h[...])
        stack = both[:, :PAIR] + (both[:, PAIR:] + dot(left_l, main_h[:MAIN, :PAIR]))
        for n, i in enumerate(group):
            inner_h, inner_l = split(stack[n * size_in:(n + 1) * size_in])
            both = dot(mix_h[...], jnp.concatenate([inner_h, inner_l], axis=1))
            outer = both[:, :PAIR] + (both[:, PAIR:] + dot(mix_l[...], inner_h))
            out_ref[:, i * WIDE:(i + 1) * WIDE] = encode(outer).reshape(FIRST, WIDE, PAIR)


def squeeze(tensor, f3, f4t, f5):
    size = R3 * DEPTH
    hbm = pl.BlockSpec(memory_space=pltpu.MemorySpace.HBM)
    return pl.pallas_call(
        squeeze_kernel,
        in_specs=[hbm] * 4,
        out_shape=pltpu.VMEM((FIRST, ROWS * WIDE, PAIR), BF16),
        out_specs=pl.BlockSpec(memory_space=pltpu.VMEM),
        scratch_shapes=[
            pltpu.VMEM((ROWS, DEPTH, CELLS), F32),
            pltpu.VMEM((I3, R3), F32),
            pltpu.VMEM((R4, I4), F32),
            pltpu.VMEM((I5, R5), F32),
            pltpu.VMEM((DEEP, 2 * PAIR), BF16),
            pltpu.VMEM((size, size), BF16),
            pltpu.VMEM((size, size), BF16),
            pltpu.SemaphoreType.DMA((ROWS + 3,)),
        ],
        compiler_params=pltpu.CompilerParams(vmem_limit_bytes=58 * 1024 * 1024),
    )(tensor, f3, f4t, f5)


def expand_kernel(x_ref, f2t_ref, out_ref, rows_ref):
    high, low = split(f2t_ref[...])
    left = jnp.concatenate([high, low], axis=0)
    for i in range(ROWS):
        code = x_ref[:, i * WIDE:(i + 1) * WIDE]
        pieces = split(decode(code).reshape(NARROW, XL, DEPTH, PAIR))
        right_h, right_l = (
            jnp.concatenate([p[:, x].reshape(NARROW * DEPTH, PAIR) for x in range(XL)], axis=1)
            for p in pieces
        )
        both = dot(left, right_h)
        core = both[:R2] + (both[R2:] + dot(left[:R2], right_l))
        for h in range(2):
            rows_ref[pl.ds(h * ROWS + i, R2, stride=2 * ROWS), :] = core[:, h * PAIR:(h + 1) * PAIR]
    out_ref[...] = rows_ref[...].astype(BF16).reshape(Z, BLOCK, PAIR)


def expand(gathered, f2t):
    return pl.pallas_call(
        expand_kernel,
        out_shape=jax.ShapeDtypeStruct((Z, BLOCK, PAIR), BF16),
        scratch_shapes=[pltpu.VMEM((R2 * 2 * ROWS, PAIR), F32)],
        compiler_params=pltpu.CompilerParams(vmem_limit_bytes=VMEM_LIMIT),
    )(gathered, f2t)


STEPS = R2 // Z // 2


def spread_rows(ref):
    row = lax.broadcasted_iota(jnp.int32, (SLICES * PAD, BLOCK), 0)
    col = lax.broadcasted_iota(jnp.int32, (SLICES * PAD, BLOCK), 1)
    spread = ((row % PAD < ROWS) & (row // PAD * ROWS + row % PAD == col)).astype(BF16)
    wide = [
        dot(spread, jnp.concatenate([ref[g], ref[g + 1]], axis=1)).astype(BF16) for g in range(0, Z, 2)
    ]
    padded = [both[:, h * PAIR:(h + 1) * PAIR] for both in wide for h in range(2)]
    span = XL * PAD
    return [
        jnp.concatenate(
            [
                jnp.concatenate([p[(2 * q + h) * span:(2 * q + h + 1) * span] for h in range(2)], axis=1)
                for p in padded
            ],
            axis=0,
        )
        for q in range(STEPS)
    ]


def outer_product(left, right):
    return lax.dot_general(left, right, (((1,), (1,)), ((), ())), preferred_element_type=F32)


def own_kernel(own_ref, left_ref, total_ref):
    rows = spread_rows(own_ref)
    for q in range(STEPS):
        left_ref[q] = rows[q]
    total_ref[...] = sum(outer_product(part, part) for part in rows)


def own_gram(own):
    size = GROUPS * PAD
    return pl.pallas_call(
        own_kernel,
        out_shape=(
            jax.ShapeDtypeStruct((STEPS, size, 2 * PAIR), BF16),
            jax.ShapeDtypeStruct((size, size), F32),
        ),
        cost_estimate=pl.CostEstimate(flops=400_000_000, bytes_accessed=1_200_000, transcendentals=0),
        compiler_params=pltpu.CompilerParams(vmem_limit_bytes=VMEM_LIMIT),
    )(own)


def gram_kernel(left_ref, own_ref, other_ref, out_ref):
    rows = spread_rows(other_ref)
    other = sum(outer_product(left_ref[q], rows[q]) for q in range(STEPS))
    own = own_ref[...]
    peak = jnp.max(jnp.maximum(jnp.abs(own), jnp.abs(other)), axis=0, keepdims=True)
    level = exponent(jnp.broadcast_to(jnp.max(peak, axis=1, keepdims=True), (8, 128)))
    factor = jnp.exp2(-level)
    lane = lax.broadcasted_iota(jnp.int32, (8, 128), 1)
    slot, mark = lane // 32, lane == PAD - 1
    for g in range(GROUPS):
        for tile in range(2):
            cols = slice(tile * 128, tile * 128 + 128)
            top, bottom = slice(g * PAD, g * PAD + 8), slice(g * PAD + 8, (g + 1) * PAD)
            parts = [
                own[top, cols] * factor,
                pltpu.roll(other[top, cols] * factor, 32, 1),
                pltpu.roll(own[bottom, cols] * factor, 64, 1),
                pltpu.roll(other[bottom, cols] * factor, 96, 1),
            ]
            for n in range(4):
                block = parts[0]
                for k in range(1, 4):
                    block = jnp.where(slot == (n + k) % 4, parts[k], block)
                out_ref[g * NARROW + tile * 4 + n] = jnp.where(mark, level, block)


def gram(left, own, other):
    return pl.pallas_call(
        gram_kernel,
        out_shape=jax.ShapeDtypeStruct((GROUPS * NARROW, 8, 128), F32),
        compiler_params=pltpu.CompilerParams(vmem_limit_bytes=VMEM_LIMIT),
    )(left, own, other)


def finish_kernel(x_ref, out_ref):
    scale = 1.0 / math.sqrt(R2 * R3 * R4 * R5)
    factor = jnp.exp2(x_ref[:, :, PAD - 1:PAD])
    total = jnp.sum(x_ref[...] * factor, axis=0) * scale
    place = lax.axis_index("y")
    turned = total
    for k in range(1, 4):
        turned = jnp.where(place == k, pltpu.roll(total, 128 - 32 * k, 1), turned)
    own = jnp.concatenate([turned[:, :32], turned[:, 64:96]], axis=0)[:ROWS]
    other = jnp.concatenate([turned[:, 32:64], turned[:, 96:]], axis=0)[:ROWS]
    group = [half[:, x * PAD:x * PAD + ROWS] for x in range(XL) for half in (own, other)]
    first = lax.axis_index("core") == 0
    out_ref[...] = jnp.where(
        first, jnp.concatenate(group, axis=1), jnp.concatenate([group[g ^ 1] for g in range(4)], axis=1)
    )


def finish(parts):
    return pl.pallas_call(
        finish_kernel,
        out_shape=jax.ShapeDtypeStruct((ROWS, 4 * ROWS), F32),
        compiler_params=pltpu.CompilerParams(vmem_limit_bytes=VMEM_LIMIT),
    )(parts)


def per_device(tensor, f2, f3, f4, f5):
    with jax.named_scope("squeeze"):
        reduced = squeeze(tensor, f3, f4.T, f5)
    with jax.named_scope("depth_exchange"):
        gathered = lax.all_to_all(reduced, ("x_hi", "y", "x_lo"), 0, 0, tiled=True)
    with jax.named_scope("expand"):
        core = expand(gathered, f2.T)
    with jax.named_scope("row_exchange"):
        rows = lax.all_to_all(core, "z", 0, 0, tiled=True)
    with jax.named_scope("core_swap"):
        other = lax.ppermute(rows, "core", [(0, 1), (1, 0)])
    with jax.named_scope("own_gram"):
        left, own = own_gram(rows)
    with jax.named_scope("gram"):
        parts = gram(left, own, other)
    with jax.named_scope("gram_exchange"):
        parts = lax.all_to_all(parts.astype(F16), ("z", "x_lo", "x_hi", "y"), 0, 0, tiled=True).astype(F32)
    with jax.named_scope("finish"):
        return finish(parts)


def solution(mesh):
    fine = Mesh(
        mesh.devices.reshape(Z, XL, CORE, XH, Y), ("z", "x_lo", "core", "x_hi", "y")
    )
    blk, narrow = ("z", "x_lo", "core"), ("x_hi", "y")
    return jax.shard_map(
        per_device,
        mesh=fine,
        in_specs=(P(blk, narrow, None), P(), P(), P(), P()),
        out_specs=P(blk, narrow),
        check_vma=False,
    )
```

```python
import math

import jax
import jax.numpy as jnp
from jax import lax
from jax.experimental import pallas as pl
from jax.experimental.pallas import tpu as pltpu
from jax.sharding import Mesh, PartitionSpec as P

F32 = jnp.float32
BF16 = jnp.bfloat16
F16 = jnp.float16
ROWS, DEPTH, I3, I4, I5 = 14, 16, 16, 33, 8
R2, R3, R4, R5 = 64, 16, 16, 8
CELLS = I3 * I4 * I5
INNER = I4 * I5
PAIR = R4 * R5
WIDE = DEPTH
PAD = 16
MAIN = 256
DEEP = 2 * INNER - MAIN
SHIFT_BITS = 24.0
SHIFT = 2.0 ** SHIFT_BITS
ROWS_STEP = 2
Z, XL, CORE, XH, Y = 8, 2, 2, 2, 4
NARROW = XH * Y
FIRST = NARROW * XL
GROUPS = Z * XL
SLICES = R2 // Z * XL
BLOCK = SLICES * ROWS
VMEM_LIMIT = 32 * 1024 * 1024


def split(value):
    high = value.astype(BF16)
    return high, (value - high.astype(F32)).astype(BF16)


def dot(left, right):
    return lax.dot_general(left, right, (((1,), (0,)), ((), ())), preferred_element_type=F32)


def exponent(peak):
    return jnp.floor(jnp.log2(jnp.maximum(peak, 1e-30))) - 14.0


def encode(value):
    wide = value * SHIFT
    return (wide * wide * wide).astype(BF16)


def decode(code):
    wide = code.astype(F32)
    power = jnp.log2(jnp.maximum(jnp.abs(wide), 1e-38))
    return wide * jnp.exp2(power * (-2.0 / 3.0) - SHIFT_BITS)


def exact_dot(left, right, dims):
    return lax.dot_general(
        left, right, (dims, ((), ())), precision=lax.Precision.HIGHEST, preferred_element_type=F32
    )


def squeeze_kernel(
    t_hbm, f3_hbm, f4t_hbm, f5_hbm, out_ref,
    t_ref, f3_ref, f4t_ref, f5_ref, main_h, mix_h, mix_l, sems,
):
    small = [
        pltpu.make_async_copy(src, dst, sems.at[ROWS + n])
        for n, (src, dst) in enumerate(
            ((f3_hbm, f3_ref), (f4t_hbm, f4t_ref), (f5_hbm, f5_ref))
        )
    ]
    loads = [pltpu.make_async_copy(t_hbm.at[i], t_ref.at[i], sems.at[i]) for i in range(ROWS)]
    for copy in small + loads:
        copy.start()
    for copy in small:
        copy.wait()

    lane = lax.broadcasted_iota(jnp.int32, (R4, PAIR), 1)
    row = lax.broadcasted_iota(jnp.int32, (R4, PAIR), 0)
    spread_four = (lane // R5 == row).astype(F32)
    lane = lax.broadcasted_iota(jnp.int32, (R5, PAIR), 1)
    row = lax.broadcasted_iota(jnp.int32, (R5, PAIR), 0)
    spread_five = (lane % R5 == row).astype(F32)
    four = exact_dot(f4t_ref[...], spread_four, ((0,), (0,)))
    five = exact_dot(f5_ref[...], spread_five, ((1,), (0,)))
    pair = (four[:, None, :] * five[None, :, :]).reshape(INNER, PAIR)
    high, low = split(pair)
    high, low = high.astype(F32), low.astype(F32)
    main_h[:, :PAIR] = jnp.concatenate([high, high[MAIN:]], axis=0).astype(BF16)
    main_h[:, PAIR:] = jnp.concatenate([low, jnp.zeros_like(low[MAIN:])], axis=0).astype(BF16)
    size = R3 * DEPTH
    a_row = lax.broadcasted_iota(jnp.int32, (size, I3), 0) // DEPTH
    a_col = lax.broadcasted_iota(jnp.int32, (size, I3), 1)
    pick = (a_row == a_col).astype(F32)
    rows = exact_dot(pick, f3_ref[...], ((1,), (1,)))
    full = exact_dot(rows, pick, ((1,), (1,)))
    same = (
        lax.broadcasted_iota(jnp.int32, (size, size), 0) % DEPTH
        == lax.broadcasted_iota(jnp.int32, (size, size), 1) % DEPTH
    )
    high, low = split(jnp.where(same, full, 0.0))
    mix_h[...] = high
    mix_l[...] = low

    size_in = R3 * DEPTH
    for base in range(0, ROWS, 7):
        group = range(base, base + 7)
        for i in group:
            loads[i].wait()
        halves = [split(t_ref[i]) for i in group]
        starts = [a * INNER for a in range(I3)]
        left_h = jnp.concatenate(
            [
                jnp.concatenate([h[:, s:s + INNER], l[:, s + MAIN:s + INNER]], axis=1)
                for h, l in halves
                for s in starts
            ],
            axis=0,
        )
        left_l = jnp.concatenate([l[:, s:s + MAIN] for _, l in halves for s in starts], axis=0)
        both = dot(left_h, main_h[...])
        stack = both[:, :PAIR] + (both[:, PAIR:] + dot(left_l, main_h[:MAIN, :PAIR]))
        inner_h, inner_l = split(stack)
        wide_h, wide_l = (
            jnp.concatenate([p[n * size_in:(n + 1) * size_in] for n in range(len(group))], axis=1)
            for p in (inner_h, inner_l)
        )
        outer = dot(
            jnp.concatenate([mix_h[...], mix_l[...], mix_h[...]], axis=1),
            jnp.concatenate([wide_h, wide_h, wide_l], axis=0),
        )
        for n, i in enumerate(group):
            out_ref[:, i * WIDE:(i + 1) * WIDE] = encode(outer[:, n * PAIR:(n + 1) * PAIR]).reshape(FIRST, WIDE, PAIR)


def squeeze(tensor, f3, f4t, f5):
    size = R3 * DEPTH
    hbm = pl.BlockSpec(memory_space=pltpu.MemorySpace.HBM)
    return pl.pallas_call(
        squeeze_kernel,
        in_specs=[hbm] * 4,
        out_shape=pltpu.VMEM((FIRST, ROWS * WIDE, PAIR), BF16),
        out_specs=pl.BlockSpec(memory_space=pltpu.VMEM),
        scratch_shapes=[
            pltpu.VMEM((ROWS, DEPTH, CELLS), F32),
            pltpu.VMEM((I3, R3), F32),
            pltpu.VMEM((R4, I4), F32),
            pltpu.VMEM((I5, R5), F32),
            pltpu.VMEM((DEEP, 2 * PAIR), BF16),
            pltpu.VMEM((size, size), BF16),
            pltpu.VMEM((size, size), BF16),
            pltpu.SemaphoreType.DMA((ROWS + 3,)),
        ],
        compiler_params=pltpu.CompilerParams(vmem_limit_bytes=58 * 1024 * 1024),
    )(tensor, f3, f4t, f5)


def expand_kernel(x_ref, f2t_ref, out_ref, rows_ref):
    high, low = split(f2t_ref[...])
    left = jnp.concatenate([high, low], axis=0)
    for i in range(ROWS):
        code = x_ref[:, i * WIDE:(i + 1) * WIDE]
        pieces = split(decode(code).reshape(NARROW, XL, DEPTH, PAIR))
        right_h, right_l = (
            jnp.concatenate([p[:, x].reshape(NARROW * DEPTH, PAIR) for x in range(XL)], axis=1)
            for p in pieces
        )
        both = dot(left, right_h)
        core = both[:R2] + (both[R2:] + dot(left[:R2], right_l))
        for h in range(2):
            rows_ref[pl.ds(h * ROWS + i, R2, stride=2 * ROWS), :] = core[:, h * PAIR:(h + 1) * PAIR]
    out_ref[...] = rows_ref[...].astype(BF16).reshape(Z, BLOCK, PAIR)


def expand(gathered, f2t):
    return pl.pallas_call(
        expand_kernel,
        out_shape=jax.ShapeDtypeStruct((Z, BLOCK, PAIR), BF16),
        scratch_shapes=[pltpu.VMEM((R2 * 2 * ROWS, PAIR), F32)],
        compiler_params=pltpu.CompilerParams(vmem_limit_bytes=VMEM_LIMIT),
    )(gathered, f2t)


STEPS = R2 // Z // 2


def spread_rows(ref):
    row = lax.broadcasted_iota(jnp.int32, (SLICES * PAD, BLOCK), 0)
    col = lax.broadcasted_iota(jnp.int32, (SLICES * PAD, BLOCK), 1)
    spread = ((row % PAD < ROWS) & (row // PAD * ROWS + row % PAD == col)).astype(BF16)
    wide = [
        dot(spread, jnp.concatenate([ref[g], ref[g + 1]], axis=1)).astype(BF16) for g in range(0, Z, 2)
    ]
    padded = [both[:, h * PAIR:(h + 1) * PAIR] for both in wide for h in range(2)]
    span = XL * PAD
    return [
        jnp.concatenate(
            [
                jnp.concatenate([p[(2 * q + h) * span:(2 * q + h + 1) * span] for h in range(2)], axis=1)
                for p in padded
            ],
            axis=0,
        )
        for q in range(STEPS)
    ]


def outer_product(left, right):
    return lax.dot_general(left, right, (((1,), (1,)), ((), ())), preferred_element_type=F32)


def own_kernel(own_ref, left_ref, total_ref):
    rows = spread_rows(own_ref)
    for q in range(STEPS):
        left_ref[q] = rows[q]
    total_ref[...] = sum(outer_product(part, part) for part in rows)


def own_gram(own):
    size = GROUPS * PAD
    return pl.pallas_call(
        own_kernel,
        out_shape=(
            jax.ShapeDtypeStruct((STEPS, size, 2 * PAIR), BF16),
            jax.ShapeDtypeStruct((size, size), F32),
        ),
        cost_estimate=pl.CostEstimate(flops=400_000_000, bytes_accessed=1_200_000, transcendentals=0),
        compiler_params=pltpu.CompilerParams(vmem_limit_bytes=VMEM_LIMIT),
    )(own)


def gram_kernel(left_ref, own_ref, other_ref, out_ref):
    rows = spread_rows(other_ref)
    other = sum(outer_product(left_ref[q], rows[q]) for q in range(STEPS))
    own = own_ref[...]
    peak = jnp.max(jnp.maximum(jnp.abs(own), jnp.abs(other)), axis=0, keepdims=True)
    level = exponent(jnp.broadcast_to(jnp.max(peak, axis=1, keepdims=True), (8, 128)))
    factor = jnp.exp2(-level)
    lane = lax.broadcasted_iota(jnp.int32, (8, 128), 1)
    slot, mark = lane // 32, lane == PAD - 1
    for g in range(GROUPS):
        for tile in range(2):
            cols = slice(tile * 128, tile * 128 + 128)
            top, bottom = slice(g * PAD, g * PAD + 8), slice(g * PAD + 8, (g + 1) * PAD)
            parts = [
                own[top, cols] * factor,
                pltpu.roll(other[top, cols] * factor, 32, 1),
                pltpu.roll(own[bottom, cols] * factor, 64, 1),
                pltpu.roll(other[bottom, cols] * factor, 96, 1),
            ]
            for n in range(4):
                block = parts[0]
                for k in range(1, 4):
                    block = jnp.where(slot == (n + k) % 4, parts[k], block)
                out_ref[g * NARROW + tile * 4 + n] = jnp.where(mark, level, block)


def gram(left, own, other):
    return pl.pallas_call(
        gram_kernel,
        out_shape=jax.ShapeDtypeStruct((GROUPS * NARROW, 8, 128), F32),
        compiler_params=pltpu.CompilerParams(vmem_limit_bytes=VMEM_LIMIT),
    )(left, own, other)


def finish_kernel(x_ref, out_ref):
    scale = 1.0 / math.sqrt(R2 * R3 * R4 * R5)
    factor = jnp.exp2(x_ref[:, :, PAD - 1:PAD])
    total = jnp.sum(x_ref[...] * factor, axis=0) * scale
    place = lax.axis_index("y")
    turned = total
    for k in range(1, 4):
        turned = jnp.where(place == k, pltpu.roll(total, 128 - 32 * k, 1), turned)
    own = jnp.concatenate([turned[:, :32], turned[:, 64:96]], axis=0)[:ROWS]
    other = jnp.concatenate([turned[:, 32:64], turned[:, 96:]], axis=0)[:ROWS]
    group = [half[:, x * PAD:x * PAD + ROWS] for x in range(XL) for half in (own, other)]
    first = lax.axis_index("core") == 0
    out_ref[...] = jnp.where(
        first, jnp.concatenate(group, axis=1), jnp.concatenate([group[g ^ 1] for g in range(4)], axis=1)
    )


def finish(parts):
    return pl.pallas_call(
        finish_kernel,
        out_shape=jax.ShapeDtypeStruct((ROWS, 4 * ROWS), F32),
        compiler_params=pltpu.CompilerParams(vmem_limit_bytes=VMEM_LIMIT),
    )(parts)


def per_device(tensor, f2, f3, f4, f5):
    with jax.named_scope("squeeze"):
        reduced = squeeze(tensor, f3, f4.T, f5)
    with jax.named_scope("depth_exchange"):
        gathered = lax.all_to_all(reduced, ("x_hi", "y", "x_lo"), 0, 0, tiled=True)
    with jax.named_scope("expand"):
        core = expand(gathered, f2.T)
    with jax.named_scope("row_exchange"):
        rows = lax.all_to_all(core, "z", 0, 0, tiled=True)
    with jax.named_scope("core_swap"):
        other = lax.ppermute(rows, "core", [(0, 1), (1, 0)])
    with jax.named_scope("own_gram"):
        left, own = own_gram(rows)
    with jax.named_scope("gram"):
        parts = gram(left, own, other)
    with jax.named_scope("gram_exchange"):
        parts = lax.all_to_all(parts.astype(F16), ("z", "x_lo", "x_hi", "y"), 0, 0, tiled=True).astype(F32)
    with jax.named_scope("finish"):
        return finish(parts)


def solution(mesh):
    fine = Mesh(
        mesh.devices.reshape(Z, XL, CORE, XH, Y), ("z", "x_lo", "core", "x_hi", "y")
    )
    blk, narrow = ("z", "x_lo", "core"), ("x_hi", "y")
    return jax.shard_map(
        per_device,
        mesh=fine,
        in_specs=(P(blk, narrow, None), P(), P(), P(), P()),
        out_specs=P(blk, narrow),
        check_vma=False,
    )
```
